256 devices in a mesh: seq: 64 (over y, z_lo, x), head: 4 (over z_hi, core).
Axes of the slice: x: 4, y: 4, z: 8 (z_hi: 2, z_lo: 4; z = z_hi * 4 + z_lo), core: 2. Of those that a mesh axis runs over, the one named last changes fastest.
Arguments:
- queries: bfloat16 [16384, 1024], P('seq', 'head'), may hold values from -16 to 16
- key_states: bfloat16 [16384, 1024], P('seq', 'head'), may hold values from -16 to 16
- value_states: bfloat16 [16384, 1024], P('seq', 'head'), may hold values from -6 to 6
- cotangent: bfloat16 [16384, 1024], P('seq', 'head'), may hold values from -6 to 6
- out_weight: bfloat16 [1024, 1024], P('head'), may hold values from -0.1875 to 0.1875
- partner: int32 [64], replicated, may hold values from 0 to 63, as said below
- counts: int32 [64], replicated, may hold values from 128 to 256, as said below
Outputs:
- layer_out: bfloat16 [16384, 1024], P('seq', 'head')
- grad_query: bfloat16 [16384, 1024], P('seq', 'head')
- grad_key: bfloat16 [16384, 1024], P('seq', 'head')
- grad_value: bfloat16 [16384, 1024], P('seq', 'head')
The draws below stay inside these ranges and needn't reach their ends.
Inputs may be any that keep to these rules, and one draw needn't show every extreme that they name: partner[b] = b XOR r for one r of 1 to 63, the same r for every block; so partner[partner[b]] = b and no block is its own partner. The valid frames of a block are its first counts[b] frames.
All inputs are finite; a program needn't handle non-finite values.
Results may differ from the reference program's by a relative error of at most 0.024.
Values may be sent and summed in bfloat16 or wider, within the bound.
A program may use at most 64 MiB of HBM per device.

```python
import jax
import jax.numpy as jnp
from jax import lax

D = 1024
HEADS = 16
HD = 64
FB = 256
BLOCKS = 64
TOKENS = 16384


def draw_queries(key, part):
    key = jax.random.fold_in(key, 31)
    values_drawn = jax.random.truncated_normal(key, -4.0, 4.0, (BLOCKS, FB, D), jnp.float32)
    return values_drawn.reshape(TOKENS, D).astype(jnp.bfloat16)


def draw_key_states(key, part):
    key = jax.random.fold_in(key, 47)
    values_drawn = jax.random.truncated_normal(key, -4.0, 4.0, (BLOCKS, FB, D), jnp.float32)
    return values_drawn.reshape(TOKENS, D).astype(jnp.bfloat16)


def draw_partner(key, part):
    key = jax.random.fold_in(key, 11)
    xor_value = jax.random.randint(key, (), 1, BLOCKS)
    return jnp.bitwise_xor(jnp.arange(BLOCKS, dtype=jnp.int32), xor_value).astype(jnp.int32)


def draw_counts(key, part):
    key = jax.random.fold_in(key, 12)
    count_key, order_key = jax.random.split(key)
    drawn = jax.random.randint(count_key, (BLOCKS,), FB // 2, FB + 1)
    order = jax.random.permutation(order_key, BLOCKS)
    drawn = drawn.at[order[0]].set(FB).at[order[1]].set(FB // 2)
    return drawn.astype(jnp.int32)


def level_of(stream_key, shape, shards, low, largest):
    loudness = 1.0
    for position, parts in shards:
        steps = jax.random.uniform(jax.random.fold_in(jax.random.fold_in(stream_key, 6), position), (parts,), jnp.float32, low / len(shards), largest / len(shards))
        loudness = loudness * jnp.repeat(jnp.exp(steps), shape[position] // parts).reshape((-1,) + (1,) * (len(shape) - 1 - position))
    return loudness


def normal_values(stream_key, extent, width, bound, cuts=(), kind=jnp.bfloat16):
    result = jax.random.normal(stream_key, extent, jnp.float32) * width
    if len(cuts) > 0:
        result = level_of(stream_key, extent, cuts, -0.22, 0.18) * result
    return jnp.clip(result, min=-bound, max=bound).astype(kind)


def setup_inputs(seed: int = 0) -> dict:
    splits = jax.random.split(jax.random.key(seed), 8)
    queries = draw_queries(jax.random.fold_in(splits[7], 71), 0)
    key_states = draw_key_states(jax.random.fold_in(splits[7], 71), 0)
    value_states = normal_values(splits[2], (TOKENS, D), 1.0, 6.0, ((0, 64), (1, 4)))
    cotangent = normal_values(splits[3], (TOKENS, D), 1.0, 6.0, ((0, 64), (1, 4)))
    out_weight = normal_values(splits[4], (D, D), D ** -0.5, 0.1875, ((0, 4),))
    partner = draw_partner(jax.random.fold_in(splits[7], 71), 0)
    counts = draw_counts(jax.random.fold_in(splits[7], 71), 0)
    return dict(queries=queries, key_states=key_states, value_states=value_states, cotangent=cotangent, out_weight=out_weight, partner=partner, counts=counts)


masked_score = -1.0e30


def reference(queries, key_states, value_states, cotangent, out_weight, partner, counts):
    score_scale = HD ** -0.5
    query_blocks = queries.reshape(BLOCKS, FB, HEADS, HD)
    key_blocks = key_states.reshape(BLOCKS, FB, HEADS, HD)
    value_blocks = value_states.reshape(BLOCKS, FB, HEADS, HD)
    positions = jnp.arange(FB, dtype=jnp.int32)
    block_valid = positions[None, :] < counts[:, None]

    def gather_set(index):
        other = partner[index]
        keys_set = jnp.concatenate([key_blocks[index], key_blocks[other]], axis=0).astype(jnp.float32)
        values_set = jnp.concatenate([value_blocks[index], value_blocks[other]], axis=0).astype(jnp.float32)
        valid_set = jnp.concatenate([block_valid[index], block_valid[other]], axis=0)
        return keys_set, values_set, valid_set

    def softmax_block(query_rows, keys_set, valid_set):
        scores = jnp.einsum("qhd,khd->hqk", query_rows, keys_set) * score_scale
        scores = jnp.where(valid_set[None, None, :], scores, masked_score)
        row_max = jnp.max(scores, axis=2, keepdims=True)
        exponent = jnp.exp(scores - row_max)
        return exponent / jnp.sum(exponent, axis=2, keepdims=True)

    def forward_block(index):
        keys_set, values_set, valid_set = gather_set(index)
        probs = softmax_block(query_blocks[index].astype(jnp.float32), keys_set, valid_set)
        probs_bf = lax.optimization_barrier(probs.astype(jnp.bfloat16)).astype(jnp.float32)
        return jnp.einsum("hqk,khd->qhd", probs_bf, values_set).astype(jnp.bfloat16)

    indices = jnp.arange(BLOCKS, dtype=jnp.int32)
    attention = lax.map(forward_block, indices).reshape(TOKENS, D)
    layer_out = jnp.dot(attention, out_weight, preferred_element_type=jnp.float32).astype(jnp.bfloat16)
    grad_attention = jnp.dot(cotangent, out_weight.T, preferred_element_type=jnp.float32).astype(jnp.bfloat16)
    grad_blocks = grad_attention.reshape(BLOCKS, FB, HEADS, HD)
    attn_blocks = attention.reshape(BLOCKS, FB, HEADS, HD)

    def backward_block(index):
        keys_set, values_set, valid_set = gather_set(index)
        query_rows = query_blocks[index].astype(jnp.float32)
        probs = softmax_block(query_rows, keys_set, valid_set)
        probs_bf = lax.optimization_barrier(probs.astype(jnp.bfloat16)).astype(jnp.float32)
        grad_rows = grad_blocks[index].astype(jnp.float32)
        row_delta = jnp.sum(grad_rows * attn_blocks[index].astype(jnp.float32), axis=2)
        grad_probs = jnp.einsum("qhd,khd->hqk", grad_rows, values_set)
        grad_scores = probs * (grad_probs - row_delta.T[:, :, None])
        scores_bf = lax.optimization_barrier(grad_scores.astype(jnp.bfloat16)).astype(jnp.float32)
        grad_rows_query = (score_scale * jnp.einsum("hqk,khd->qhd", scores_bf, keys_set)).astype(jnp.bfloat16)
        key_part = score_scale * jnp.einsum("hqk,qhd->khd", scores_bf, query_rows)
        value_part = jnp.einsum("hqk,qhd->khd", probs_bf, grad_rows)
        return grad_rows_query, key_part[:FB], key_part[FB:], value_part[:FB], value_part[FB:]

    grad_query, key_own, key_cross, value_own, value_cross = lax.map(backward_block, indices)
    grad_key = (key_own + key_cross[partner]).astype(jnp.bfloat16).reshape(TOKENS, D)
    grad_value = (value_own + value_cross[partner]).astype(jnp.bfloat16).reshape(TOKENS, D)
    return layer_out, grad_query.reshape(TOKENS, D), grad_key, grad_value
```

```python
import functools

import jax
import jax.numpy as jnp
from jax import lax
from jax.experimental import pallas as pl
from jax.experimental.pallas import tpu as pltpu
from jax.sharding import PartitionSpec as P

HD = 64
MESH = pl.DeviceIdType.MESH
MASKED = -1e30
BF = jnp.bfloat16
F32 = jnp.float32


def flip(index, offset):
    result = index
    for bit in range(offset.bit_length()):
        if offset >> bit & 1:
            result = result + (1 << bit) * (1 - 2 * ((index // (1 << bit)) % 2))
    return result


def dot(a, b):
    return jnp.dot(a, b, preferred_element_type=F32)


def dot_nt(a, b):
    return lax.dot_general(a, b, (((1,), (1,)), ((), ())), preferred_element_type=F32)


def kernel(
    offset, q_ref, k_ref, v_ref, cot_ref, w_ref, counts_ref,
    lo_ref, dq_ref, dk_ref, dv_ref,
    mate_kv, cots, q_stack, g_stack, k_t, v_t, probs, probs_bf, grads_bf, attn_t, dq_t,
    g_sum, part_own, part_far, part_out, part_in, far_out, far_in,
    cross_out, cross_in, send_sem, recv_sem,
):
    rows, width = q_ref.shape
    heads = width // HD
    b = lax.axis_index("seq")
    h = lax.axis_index("head")
    mate = flip(b, offset)
    peer = h + 1 - 2 * (h % 2)
    far = (h + 2) % 4
    far_peer = 3 - h
    to_mate, to_peer, to_far = (mate, h), (b, peer), (b, far)

    barrier = pltpu.get_barrier_semaphore()
    for target in (to_mate, to_peer, to_far):
        pl.semaphore_signal(barrier, inc=1, device_id=target, device_id_type=MESH)
    pl.semaphore_wait(barrier, 3)

    def copy(slot, source, landing, target):
        return pltpu.make_async_remote_copy(
            src_ref=source, dst_ref=landing, send_sem=send_sem.at[slot],
            recv_sem=recv_sem.at[slot], device_id=target, device_id_type=MESH,
        )

    def columns(group):
        return pl.ds(pl.multiple_of(group * width, width), width)

    send_k = copy(0, k_ref, mate_kv.at[0], to_mate)
    send_v = copy(1, v_ref, mate_kv.at[1], to_mate)
    send_cot_far = copy(2, cot_ref, cots.at[0], to_far)
    send_cot_peer = copy(3, cot_ref, cots.at[1], to_peer)
    forward_cot = copy(4, cots.at[0], cots.at[2], to_peer)
    send_part_far = copy(5, part_out.at[0], part_in.at[0], to_peer)
    send_part_peer = copy(6, part_out.at[1], part_in.at[1], to_peer)
    send_far = copy(7, far_out, far_in, to_far)
    send_dv = copy(8, cross_out.at[1], cross_in.at[1], to_mate)
    send_dk = copy(9, cross_out.at[0], cross_in.at[0], to_mate)

    send_k.start()
    send_v.start()
    send_cot_far.start()
    send_cot_peer.start()

    lane_head = lax.broadcasted_iota(jnp.int32, (1, width), 1) // HD
    q_scaled = q_ref[...] * jnp.asarray(HD**-0.5, BF)
    for head in range(heads):
        mask = jnp.where(lane_head == head, 1.0, 0.0).astype(BF)
        q_stack[head * rows : (head + 1) * rows, :] = q_scaled * mask
    k_t[:, :rows] = k_ref[...].T
    v_t[:, :rows] = v_ref[...].T
    key_row = lax.broadcasted_iota(jnp.int32, (rows, rows), 0)
    own_valid = key_row < counts_ref[b]
    mate_valid = key_row < counts_ref[mate]

    def head_rows(head):
        return pl.ds(pl.multiple_of(head * rows, rows), rows)

    def own_scores(head, carry):
        scores = dot_nt(k_ref[...], q_stack[head_rows(head), :])
        probs[head, :rows, :] = jnp.where(own_valid, scores, MASKED)
        return carry

    lax.fori_loop(0, heads, own_scores, 0)
    send_cot_peer.wait_recv()
    g_sum[...] = dot_nt(cot_ref[...], w_ref[:, columns(h)]) + dot_nt(
        cots[1], w_ref[:, columns(peer)]
    )

    send_k.wait_recv()
    send_v.wait_recv()
    k_t[:, rows:] = mate_kv[0].T
    v_t[:, rows:] = mate_kv[1].T

    def forward(head, carry):
        own = probs[head, :rows, :]
        other = jnp.where(mate_valid, dot_nt(mate_kv[0], q_stack[head_rows(head), :]), MASKED)
        top = jnp.maximum(
            jnp.max(own, axis=0, keepdims=True), jnp.max(other, axis=0, keepdims=True)
        )
        own = jnp.exp(own - top)
        other = jnp.exp(other - top)
        total = jnp.sum(own, axis=0, keepdims=True) + jnp.sum(other, axis=0, keepdims=True)
        inverse = 1.0 / total
        own = own * inverse
        other = other * inverse
        probs[head, :rows, :] = own
        probs[head, rows:, :] = other
        probs_bf[:rows, head_rows(head)] = own.astype(BF)
        probs_bf[rows:, head_rows(head)] = other.astype(BF)
        lanes = pl.ds(pl.multiple_of(head * HD, HD), HD)
        attn_t[lanes, :] = dot(v_t[lanes, :], probs_bf[:, head_rows(head)]).astype(BF)
        return carry

    lax.fori_loop(0, heads, forward, 0)

    attention = attn_t[...].T
    part_out[0] = dot(attention, w_ref[:, columns(far_peer)]).astype(BF)
    send_part_far.start()
    send_cot_far.wait_recv()
    forward_cot.start()
    part_out[1] = dot(attention, w_ref[:, columns(peer)]).astype(BF)
    send_part_peer.start()
    part_far[...] = dot(attention, w_ref[:, columns(far)])
    part_own[...] = dot(attention, w_ref[:, columns(h)])
    send_part_far.wait_recv()
    far_out[...] = (part_far[...] + part_in[0].astype(F32)).astype(BF)
    send_far.start()

    g_sum[...] += dot_nt(cots[0], w_ref[:, columns(far)])
    forward_cot.wait_recv()
    grad_attention = (g_sum[...] + dot_nt(cots[2], w_ref[:, columns(far_peer)])).astype(BF)
    for head in range(heads):
        mask = jnp.where(lane_head == head, 1.0, 0.0).astype(BF)
        g_stack[head * rows : (head + 1) * rows, :] = grad_attention * mask
    cross_out[1] = dot(probs_bf[rows:, :], g_stack[...]).astype(BF)
    send_dv.start()
    products = grad_attention.T.astype(F32) * attn_t[...].astype(F32)
    delta = jnp.sum(products.reshape(heads, HD, rows), axis=1)
    g_sum[:heads, :] = delta

    def score_grads(half, values):
        def step(head, carry):
            keys = slice(half * rows, (half + 1) * rows)
            grad_probs = dot_nt(values[...], g_stack[head_rows(head), :])
            grads = probs[head, keys, :] * (grad_probs - g_sum[pl.ds(head, 1), :])
            grads_bf[keys, head_rows(head)] = grads.astype(BF)
            return carry

        lax.fori_loop(0, heads, step, 0)

    score_grads(1, mate_kv.at[1])
    cross_out[0] = dot(grads_bf[rows:, :], q_stack[...]).astype(BF)
    send_dk.start()
    score_grads(0, v_ref)

    def query_grads(head, carry):
        lanes = pl.ds(pl.multiple_of(head * HD, HD), HD)
        grads = dot(k_t[lanes, :], grads_bf[:, head_rows(head)])
        dq_t[lanes, :] = (grads * HD**-0.5).astype(BF)
        return carry

    lax.fori_loop(0, heads, query_grads, 0)
    dq_ref[...] = dq_t[...].T
    own_dk = dot(grads_bf[:rows, :], q_stack[...])
    probs[0, :rows, :] = own_dk
    own_dv = dot(probs_bf[:rows, :], g_stack[...])
    probs[0, rows:, :] = own_dv

    send_part_peer.wait_recv()
    part_own[...] += part_in[1].astype(F32)
    send_far.wait_recv()
    lo_ref[...] = (part_own[...] + far_in[...].astype(F32)).astype(BF)
    send_dv.wait_recv()
    dv_ref[...] = (probs[0, rows:, :] + cross_in[1].astype(F32)).astype(BF)
    send_dk.wait_recv()
    dk_ref[...] = (probs[0, :rows, :] + cross_in[0].astype(F32)).astype(BF)
    for sent in (
        send_k, send_v, send_cot_far, send_cot_peer, forward_cot,
        send_part_far, send_part_peer, send_far, send_dv, send_dk,
    ):
        sent.wait_send()


def call(offset, queries, key_states, value_states, cotangent, out_weight, counts):
    rows, width = queries.shape
    heads = width // HD
    square = jax.ShapeDtypeStruct((rows, width), BF)
    vmem = pl.BlockSpec(memory_space=pltpu.VMEM)
    scratch = [
        pltpu.VMEM((2, rows, width), BF),
        pltpu.VMEM((3, rows, width), BF),
        pltpu.VMEM((heads * rows, width), BF),
        pltpu.VMEM((heads * rows, width), BF),
        pltpu.VMEM((width, 2 * rows), BF),
        pltpu.VMEM((width, 2 * rows), BF),
        pltpu.VMEM((heads, 2 * rows, rows), F32),
        pltpu.VMEM((2 * rows, heads * rows), BF),
        pltpu.VMEM((2 * rows, heads * rows), BF),
        pltpu.VMEM((width, rows), BF),
        pltpu.VMEM((width, rows), BF),
        pltpu.VMEM((rows, width), F32),
        pltpu.VMEM((rows, width), F32),
        pltpu.VMEM((rows, width), F32),
        pltpu.VMEM((2, rows, width), BF),
        pltpu.VMEM((2, rows, width), BF),
        pltpu.VMEM((rows, width), BF),
        pltpu.VMEM((rows, width), BF),
        pltpu.VMEM((2, rows, width), BF),
        pltpu.VMEM((2, rows, width), BF),
        pltpu.SemaphoreType.DMA((10,)),
        pltpu.SemaphoreType.DMA((10,)),
    ]
    return pl.pallas_call(
        functools.partial(kernel, offset),
        out_shape=(square,) * 4,
        in_specs=[vmem] * 5 + [pl.BlockSpec(memory_space=pltpu.SMEM)],
        out_specs=(vmem,) * 4,
        scratch_shapes=scratch,
        compiler_params=pltpu.CompilerParams(
            collective_id=offset, has_side_effects=True, vmem_limit_bytes=32 << 20
        ),
        cost_estimate=pl.CostEstimate(flops=600_000_000, bytes_accessed=2 << 20, transcendentals=524288),
    )(queries, key_states, value_states, cotangent, out_weight, counts)


OFFSETS = None


def solution(mesh):
    offsets = OFFSETS or range(1, mesh.shape["seq"])

    def per_device(queries, key_states, value_states, cotangent, out_weight, partner, counts):
        branches = [functools.partial(call, offset) for offset in offsets]
        operands = (queries, key_states, value_states, cotangent, out_weight, counts)
        if len(branches) == 1:
            return branches[0](*operands)
        return lax.switch(partner[0] - 1, branches, *operands)

    return jax.shard_map(
        per_device,
        mesh=mesh,
        in_specs=(
            P("seq", "head"), P("seq", "head"), P("seq", "head"), P("seq", "head"),
            P("head", None), P(), P(),
        ),
        out_specs=(P("seq", "head"),) * 4,
        check_vma=False,
    )
```

```python
import functools

import jax
import jax.numpy as jnp
from jax import lax
from jax.experimental import pallas as pl
from jax.experimental.pallas import tpu as pltpu
from jax.sharding import PartitionSpec as P

HD = 64
MESH = pl.DeviceIdType.MESH
MASKED = -1e30
BF = jnp.bfloat16
F32 = jnp.float32


def flip(index, offset):
    result = index
    for bit in range(offset.bit_length()):
        if offset >> bit & 1:
            result = result + (1 << bit) * (1 - 2 * ((index // (1 << bit)) % 2))
    return result


def dot(a, b):
    return jnp.dot(a, b, preferred_element_type=F32)


def dot_nt(a, b):
    return lax.dot_general(a, b, (((1,), (1,)), ((), ())), preferred_element_type=F32)


def remote(source, landing, send_sem, recv_sem, target):
    return pltpu.make_async_remote_copy(
        src_ref=source, dst_ref=landing, send_sem=send_sem, recv_sem=recv_sem,
        device_id=target, device_id_type=MESH,
    )


def swap_kernel(
    base, a_ref, b_ref, a_in, b_in, a_relayed, b_relayed, send_sem, recv_sem, relay_send, relay_recv
):
    rows = a_ref.shape[0] // PIECES
    b, h = lax.axis_index("seq"), lax.axis_index("head")
    mate, side = (flip(b, base), h), (flip(b, 1), h)
    barrier = pltpu.get_barrier_semaphore()
    targets = (mate, side) if base else (side,)
    for target in targets:
        pl.semaphore_signal(barrier, inc=1, device_id=target, device_id_type=MESH)
    pl.semaphore_wait(barrier, len(targets))
    direct, relay = [], []
    for array, refs in enumerate(((a_ref, a_in, a_relayed), (b_ref, b_in, b_relayed))):
        for piece in range(PIECES):
            slot = array * PIECES + piece
            source, landing, onward = (ref.at[pl.ds(piece * rows, rows)] for ref in refs)
            if base:
                direct.append(remote(source, landing, send_sem.at[slot], recv_sem.at[slot], mate))
            relay.append(
                remote(
                    landing if base else source, onward, relay_send.at[slot], relay_recv.at[slot],
                    side,
                )
            )
    for copy in direct:
        copy.start()
    for slot, copy in enumerate(relay):
        if base:
            direct[slot].wait_recv()
        copy.start()
    for copy in direct:
        copy.wait_send()
    for copy in relay:
        copy.wait()


def swap(base, first_id, a, b):
    anywhere = pl.BlockSpec(memory_space=pl.ANY)
    shapes = [jax.ShapeDtypeStruct(x.shape, x.dtype) for x in (a, b)]
    return pl.pallas_call(
        functools.partial(swap_kernel, base),
        out_shape=shapes * 2,
        in_specs=[anywhere] * 2,
        out_specs=[anywhere] * 4,
        scratch_shapes=[pltpu.SemaphoreType.DMA((2 * PIECES,))] * 4,
        compiler_params=pltpu.CompilerParams(
            collective_id=first_id + base // 2, has_side_effects=True, vmem_limit_bytes=2 << 20
        ),
    )(a, b)


def swap_any(partner, first_id, a, b):
    pairs = partner.shape[0] // 2
    branches = [
        functools.partial(swap, 2 * pair + pair % 2, first_id) for pair in range(pairs)
    ]
    return lax.switch(partner[0] // 2, branches, a, b)


def choose(partner_ref, direct, relayed):
    offset = partner_ref[0]
    return jnp.where((offset + offset // 2) % 2 == 0, direct[...], relayed[...])


def kernel(
    q_ref, k_ref, v_ref, k_direct, v_direct, k_relayed, v_relayed, cot_ref, w_ref, counts_ref,
    partner_ref, lo_ref, dq_ref, dk_own, dv_own, dk_cross, dv_cross,
    mate_k, mate_v, cots, q_stack, g_stack, k_t, v_t, probs, probs_bf, grads_bf, attn_t, dq_t,
    g_sum, part_own, part_far, part_out, part_in, far_out, far_in, send_sem, recv_sem,
):
    rows, width = q_ref.shape
    heads = width // HD
    b = lax.axis_index("seq")
    h = lax.axis_index("head")
    peer = h + 1 - 2 * (h % 2)
    far = (h + 2) % 4
    far_peer = 3 - h
    to_peer, to_far = (b, peer), (b, far)

    barrier = pltpu.get_barrier_semaphore()
    for target in (to_far, to_peer):
        pl.semaphore_signal(barrier, inc=1, device_id=target, device_id_type=MESH)

    def copy(slot, source, landing, target):
        return remote(source, landing, send_sem.at[slot], recv_sem.at[slot], target)

    def columns(group):
        return pl.ds(pl.multiple_of(group * width, width), width)

    send_cot_far = copy(0, cot_ref, cots.at[0], to_far)
    send_cot_peer = copy(1, cot_ref, cots.at[1], to_peer)
    forward_cot = copy(2, cots.at[0], cots.at[2], to_peer)
    send_part_far = copy(3, part_out.at[0], part_in.at[0], to_peer)
    send_part_peer = copy(4, part_out.at[1], part_in.at[1], to_peer)
    send_far = copy(5, far_out, far_in, to_far)

    mate_k[...] = choose(partner_ref, k_direct, k_relayed)
    mate_v[...] = choose(partner_ref, v_direct, v_relayed)
    lane_head = lax.broadcasted_iota(jnp.int32, (1, width), 1) // HD
    q_scaled = q_ref[...] * jnp.asarray(HD**-0.5, BF)
    for head in range(heads):
        mask = jnp.where(lane_head == head, 1.0, 0.0).astype(BF)
        q_stack[head * rows : (head + 1) * rows, :] = q_scaled * mask
    k_t[:, :rows] = k_ref[...].T
    k_t[:, rows:] = mate_k[...].T
    v_t[:, :rows] = v_ref[...].T
    v_t[:, rows:] = mate_v[...].T
    key_row = lax.broadcasted_iota(jnp.int32, (rows, rows), 0)
    own_valid = key_row < counts_ref[b]
    mate_valid = key_row < counts_ref[partner_ref[b]]

    def head_rows(head):
        return pl.ds(pl.multiple_of(head * rows, rows), rows)

    def forward(head, carry):
        own = jnp.where(own_valid, dot_nt(k_ref[...], q_stack[head_rows(head), :]), MASKED)
        other = jnp.where(mate_valid, dot_nt(mate_k[...], q_stack[head_rows(head), :]), MASKED)
        top = jnp.maximum(
            jnp.max(own, axis=0, keepdims=True), jnp.max(other, axis=0, keepdims=True)
        )
        own = jnp.exp(own - top)
        other = jnp.exp(other - top)
        total = jnp.sum(own, axis=0, keepdims=True) + jnp.sum(other, axis=0, keepdims=True)
        inverse = 1.0 / total
        own = own * inverse
        other = other * inverse
        probs[head, :rows, :] = own
        probs[head, rows:, :] = other
        probs_bf[:rows, head_rows(head)] = own.astype(BF)
        probs_bf[rows:, head_rows(head)] = other.astype(BF)
        lanes = pl.ds(pl.multiple_of(head * HD, HD), HD)
        attn_t[lanes, :] = dot(v_t[lanes, :], probs_bf[:, head_rows(head)]).astype(BF)
        return carry

    lax.fori_loop(0, EARLY, forward, 0)
    pl.semaphore_wait(barrier, 2)
    send_cot_far.start()
    send_cot_peer.start()
    lax.fori_loop(EARLY, heads, forward, 0)

    attention = attn_t[...].T
    part_out[0] = dot(attention, w_ref[:, columns(far_peer)]).astype(BF)
    send_part_far.start()
    part_out[1] = dot(attention, w_ref[:, columns(peer)]).astype(BF)
    send_part_peer.start()
    part_far[...] = dot(attention, w_ref[:, columns(far)])
    part_own[...] = dot(attention, w_ref[:, columns(h)])
    send_part_far.wait_recv()
    far_out[...] = (part_far[...] + part_in[0].astype(F32)).astype(BF)
    send_far.start()
    send_cot_peer.wait_recv()
    g_sum[...] = dot_nt(cot_ref[...], w_ref[:, columns(h)]) + dot_nt(
        cots[1], w_ref[:, columns(peer)]
    )
    send_part_peer.wait_recv()
    part_own[...] += part_in[1].astype(F32)

    send_cot_far.wait_recv()
    forward_cot.start()
    g_sum[...] += dot_nt(cots[0], w_ref[:, columns(far)])
    forward_cot.wait_recv()
    grad_attention = (g_sum[...] + dot_nt(cots[2], w_ref[:, columns(far_peer)])).astype(BF)
    for head in range(heads):
        mask = jnp.where(lane_head == head, 1.0, 0.0).astype(BF)
        g_stack[head * rows : (head + 1) * rows, :] = grad_attention * mask
    products = grad_attention.T.astype(F32) * attn_t[...].astype(F32)
    g_sum[:heads, :] = jnp.sum(products.reshape(heads, HD, rows), axis=1)

    def backward(head, carry):
        delta = g_sum[pl.ds(head, 1), :]
        for half, values in enumerate((v_ref, mate_v)):
            keys = slice(half * rows, (half + 1) * rows)
            grad_probs = dot_nt(values[...], g_stack[head_rows(head), :])
            grads = probs[head, keys, :] * (grad_probs - delta)
            grads_bf[keys, head_rows(head)] = grads.astype(BF)
        lanes = pl.ds(pl.multiple_of(head * HD, HD), HD)
        grads = dot(k_t[lanes, :], grads_bf[:, head_rows(head)])
        dq_t[lanes, :] = (grads * HD**-0.5).astype(BF)
        return carry

    lax.fori_loop(0, heads, backward, 0)
    dq_ref[...] = dq_t[...].T
    dv_cross[...] = dot(probs_bf[rows:, :], g_stack[...]).astype(BF)
    dk_cross[...] = dot(grads_bf[rows:, :], q_stack[...]).astype(BF)
    dv_own[...] = dot(probs_bf[:rows, :], g_stack[...])
    dk_own[...] = dot(grads_bf[:rows, :], q_stack[...])

    send_far.wait_recv()
    lo_ref[...] = (part_own[...] + far_in[...].astype(F32)).astype(BF)
    for sent in (
        send_cot_far, send_cot_peer, forward_cot, send_part_far, send_part_peer, send_far,
    ):
        sent.wait_send()


def attend(queries, key_states, value_states, mates, cotangent, out_weight, counts, partner):
    rows, width = queries.shape
    heads = width // HD
    narrow = jax.ShapeDtypeStruct((rows, width), BF)
    wide = jax.ShapeDtypeStruct((rows, width), F32)
    vmem = pl.BlockSpec(memory_space=pltpu.VMEM)
    smem = pl.BlockSpec(memory_space=pltpu.SMEM)
    scratch = [
        pltpu.VMEM((rows, width), BF),
        pltpu.VMEM((rows, width), BF),
        pltpu.VMEM((3, rows, width), BF),
        pltpu.VMEM((heads * rows, width), BF),
        pltpu.VMEM((heads * rows, width), BF),
        pltpu.VMEM((width, 2 * rows), BF),
        pltpu.VMEM((width, 2 * rows), BF),
        pltpu.VMEM((heads, 2 * rows, rows), F32),
        pltpu.VMEM((2 * rows, heads * rows), BF),
        pltpu.VMEM((2 * rows, heads * rows), BF),
        pltpu.VMEM((width, rows), BF),
        pltpu.VMEM((width, rows), BF),
        pltpu.VMEM((rows, width), F32),
        pltpu.VMEM((rows, width), F32),
        pltpu.VMEM((rows, width), F32),
        pltpu.VMEM((2, rows, width), BF),
        pltpu.VMEM((2, rows, width), BF),
        pltpu.VMEM((rows, width), BF),
        pltpu.VMEM((rows, width), BF),
        pltpu.SemaphoreType.DMA((6,)),
        pltpu.SemaphoreType.DMA((6,)),
    ]
    return pl.pallas_call(
        kernel,
        out_shape=(narrow, narrow, wide, wide, narrow, narrow),
        in_specs=[vmem] * 9 + [smem] * 2,
        out_specs=(vmem,) * 6,
        scratch_shapes=scratch,
        compiler_params=pltpu.CompilerParams(
            collective_id=0, has_side_effects=True, vmem_limit_bytes=20 << 20
        ),
        cost_estimate=pl.CostEstimate(
            flops=600_000_000, bytes_accessed=3 << 20, transcendentals=524288
        ),
    )(queries, key_states, value_states, *mates, cotangent, out_weight, counts, partner)


def finish_kernel(
    lo, dq, dk_own, dv_own, dk_direct, dv_direct, dk_relayed, dv_relayed, partner_ref,
    lo_ref, dq_ref, dk_ref, dv_ref,
):
    lo_ref[...] = lo[...]
    dq_ref[...] = dq[...]
    dk_ref[...] = (dk_own[...] + choose(partner_ref, dk_direct, dk_relayed).astype(F32)).astype(BF)
    dv_ref[...] = (dv_own[...] + choose(partner_ref, dv_direct, dv_relayed).astype(F32)).astype(BF)


def finish(lo, dq, dk_own, dv_own, returned, partner):
    vmem = pl.BlockSpec(memory_space=pltpu.VMEM)
    smem = pl.BlockSpec(memory_space=pltpu.SMEM)
    return pl.pallas_call(
        finish_kernel,
        out_shape=(jax.ShapeDtypeStruct(lo.shape, BF),) * 4,
        in_specs=[vmem] * 8 + [smem],
        out_specs=(vmem,) * 4,
        compiler_params=pltpu.CompilerParams(vmem_limit_bytes=4 << 20),
    )(lo, dq, dk_own, dv_own, *returned, partner)


EARLY = 2
PIECES = 2


def per_device(queries, key_states, value_states, cotangent, out_weight, partner, counts):
    mates = swap_any(partner, 1, key_states, value_states)
    lo, dq, dk_own, dv_own, dk_cross, dv_cross = attend(
        queries, key_states, value_states, mates, cotangent, out_weight, counts, partner
    )
    returned = swap_any(partner, 1, dk_cross, dv_cross)
    return finish(lo, dq, dk_own, dv_own, returned, partner)


def solution(mesh):
    return jax.shard_map(
        per_device,
        mesh=mesh,
        in_specs=(
            P("seq", "head"), P("seq", "head"), P("seq", "head"), P("seq", "head"),
            P("head", None), P(), P(),
        ),
        out_specs=(P("seq", "head"),) * 4,
        check_vma=False,
    )
```

```python
import functools

import jax
import jax.numpy as jnp
from jax import lax
from jax.experimental import pallas as pl
from jax.experimental.pallas import tpu as pltpu
from jax.sharding import PartitionSpec as P

HD = 64
MESH = pl.DeviceIdType.MESH
MASKED = -1e30
BF = jnp.bfloat16
F32 = jnp.float32


def flip(index, offset):
    result = index
    for bit in range(offset.bit_length()):
        if offset >> bit & 1:
            result = result + (1 << bit) * (1 - 2 * ((index // (1 << bit)) % 2))
    return result


def dot(a, b):
    return jnp.dot(a, b, preferred_element_type=F32)


def dot_nt(a, b):
    return lax.dot_general(a, b, (((1,), (1,)), ((), ())), preferred_element_type=F32)


def remote(source, landing, send_sem, recv_sem, target):
    return pltpu.make_async_remote_copy(
        src_ref=source, dst_ref=landing, send_sem=send_sem, recv_sem=recv_sem,
        device_id=target, device_id_type=MESH,
    )


def swap_kernel(
    base, a_ref, b_ref, partner_ref, a_in, a_relayed, b_in, b_own, b_side, b_pick, partner,
    load_sem, a_send, a_recv, relay_send, relay_recv, side_send, side_recv, b_send, b_recv,
):
    rows = a_ref.shape[0] // PIECES
    b, h = lax.axis_index("seq"), lax.axis_index("head")
    mate, side = (flip(b, base), h), (flip(b, 1), h)
    targets = (mate, side) if base else (side,)
    load_b = pltpu.make_async_copy(b_ref, b_own, load_sem.at[0])
    load_partner = pltpu.make_async_copy(partner_ref, partner, load_sem.at[1])
    if base:
        load_b.start()
        load_partner.start()
    barrier = pltpu.get_barrier_semaphore()
    for target in targets:
        pl.semaphore_signal(barrier, inc=1, device_id=target, device_id_type=MESH)
    pl.semaphore_wait(barrier, len(targets))

    def pieces(source, landing, send_sem, recv_sem, target):
        return [
            remote(
                source.at[pl.ds(i * rows, rows)], landing.at[pl.ds(i * rows, rows)],
                send_sem.at[i], recv_sem.at[i], target,
            )
            for i in range(PIECES)
        ]

    relay_a = pieces(a_in if base else a_ref, a_relayed, relay_send, relay_recv, side)
    side_b = pieces(b_ref, b_side if base else b_in, side_send, side_recv, side)
    for copy in side_b:
        copy.start()
    if not base:
        for copy in relay_a:
            copy.start()
        for copy in side_b + relay_a:
            copy.wait()
        return
    direct_a = pieces(a_ref, a_in, a_send, a_recv, mate)
    picked_b = pieces(b_pick, b_in, b_send, b_recv, mate)
    for copy in direct_a:
        copy.start()
    load_b.wait()
    load_partner.wait()
    relayed = is_relayed(partner)
    for i in range(PIECES):
        side_b[i].wait_recv()
        piece = slice(i * rows, (i + 1) * rows)
        b_pick[piece, :] = jnp.where(relayed, b_side[piece, :], b_own[piece, :])
        picked_b[i].start()
    for i in range(PIECES):
        direct_a[i].wait_recv()
        relay_a[i].start()
    for copy in side_b + direct_a:
        copy.wait_send()
    for copy in picked_b + relay_a:
        copy.wait()


def swap(base, first_id, a, b, partner):
    anywhere = pl.BlockSpec(memory_space=pl.ANY)
    shapes = [jax.ShapeDtypeStruct(x.shape, x.dtype) for x in (a, a, b)]
    return pl.pallas_call(
        functools.partial(swap_kernel, base),
        out_shape=shapes,
        in_specs=[anywhere] * 3,
        out_specs=[anywhere] * 3,
        scratch_shapes=[pltpu.VMEM(b.shape, b.dtype)] * 3
        + [pltpu.SMEM(partner.shape, partner.dtype), pltpu.SemaphoreType.DMA((2,))]
        + [pltpu.SemaphoreType.DMA((PIECES,))] * 8,
        compiler_params=pltpu.CompilerParams(
            collective_id=first_id + base // 2, has_side_effects=True, vmem_limit_bytes=2 << 20
        ),
    )(a, b, partner)


def swap_any(partner, first_id, a, b):
    pairs = partner.shape[0] // 2
    branches = [
        functools.partial(swap, 2 * pair + pair % 2, first_id) for pair in range(pairs)
    ]
    return lax.switch(partner[0] // 2, branches, a, b, partner)


def is_relayed(partner_ref):
    offset = partner_ref[0]
    return (offset + offset // 2) % 2 == 1


def choose(partner_ref, direct, relayed):
    return jnp.where(is_relayed(partner_ref), relayed[...], direct[...])


def kernel(
    q_ref, k_ref, v_ref, k_direct, k_relayed, mate_v, cot_ref, w_ref, counts_ref,
    partner_ref, lo_ref, dq_ref, dk_own, dv_own, dk_cross, dv_cross,
    mate_k, cots, q_stack, g_stack, k_t, v_t, probs, probs_bf, grads_bf, attn_t, dq_t,
    g_sum, part_own, part_far, part_out, part_in, far_out, far_in, send_sem, recv_sem,
):
    rows, width = q_ref.shape
    heads = width // HD
    b = lax.axis_index("seq")
    h = lax.axis_index("head")
    peer = h + 1 - 2 * (h % 2)
    far = (h + 2) % 4
    far_peer = 3 - h
    to_peer, to_far = (b, peer), (b, far)

    barrier = pltpu.get_barrier_semaphore()
    for target in (to_far, to_peer):
        pl.semaphore_signal(barrier, inc=1, device_id=target, device_id_type=MESH)

    def copy(slot, source, landing, target):
        return remote(source, landing, send_sem.at[slot], recv_sem.at[slot], target)

    def columns(group):
        return pl.ds(pl.multiple_of(group * width, width), width)

    send_cot_far = copy(0, cot_ref, cots.at[0], to_far)
    send_cot_peer = copy(1, cot_ref, cots.at[1], to_peer)
    forward_cot = copy(2, cots.at[0], cots.at[2], to_peer)
    send_part_far = copy(3, part_out.at[0], part_in.at[0], to_peer)
    send_part_peer = copy(4, part_out.at[1], part_in.at[1], to_peer)
    send_far = copy(5, far_out, far_in, to_far)

    mate_k[...] = choose(partner_ref, k_direct, k_relayed)
    lane_head = lax.broadcasted_iota(jnp.int32, (1, width), 1) // HD
    q_scaled = q_ref[...] * jnp.asarray(HD**-0.5, BF)
    for head in range(heads):
        mask = jnp.where(lane_head == head, 1.0, 0.0).astype(BF)
        q_stack[head * rows : (head + 1) * rows, :] = q_scaled * mask
    k_t[:, :rows] = k_ref[...].T
    k_t[:, rows:] = mate_k[...].T
    v_t[:, :rows] = v_ref[...].T
    v_t[:, rows:] = mate_v[...].T
    key_row = lax.broadcasted_iota(jnp.int32, (rows, rows), 0)
    own_valid = key_row < counts_ref[b]
    mate_valid = key_row < counts_ref[partner_ref[b]]

    def head_rows(head):
        return pl.ds(pl.multiple_of(head * rows, rows), rows)

    def forward(head, carry):
        own = jnp.where(own_valid, dot_nt(k_ref[...], q_stack[head_rows(head), :]), MASKED)
        other = jnp.where(mate_valid, dot_nt(mate_k[...], q_stack[head_rows(head), :]), MASKED)
        top = jnp.maximum(
            jnp.max(own, axis=0, keepdims=True), jnp.max(other, axis=0, keepdims=True)
        )
        own = jnp.exp(own - top)
        other = jnp.exp(other - top)
        total = jnp.sum(own, axis=0, keepdims=True) + jnp.sum(other, axis=0, keepdims=True)
        inverse = 1.0 / total
        own = own * inverse
        other = other * inverse
        probs[head, :rows, :] = own
        probs[head, rows:, :] = other
        probs_bf[:rows, head_rows(head)] = own.astype(BF)
        probs_bf[rows:, head_rows(head)] = other.astype(BF)
        lanes = pl.ds(pl.multiple_of(head * HD, HD), HD)
        attn_t[lanes, :] = dot(v_t[lanes, :], probs_bf[:, head_rows(head)]).astype(BF)
        return carry

    lax.fori_loop(0, EARLY, forward, 0)
    pl.semaphore_wait(barrier, 2)
    send_cot_far.start()
    send_cot_peer.start()
    lax.fori_loop(EARLY, heads, forward, 0)

    attention = attn_t[...].T
    part_out[0] = dot(attention, w_ref[:, columns(far_peer)]).astype(BF)
    send_part_far.start()
    part_out[1] = dot(attention, w_ref[:, columns(peer)]).astype(BF)
    send_part_peer.start()
    part_far[...] = dot(attention, w_ref[:, columns(far)])
    part_own[...] = dot(attention, w_ref[:, columns(h)])
    send_part_far.wait_recv()
    far_out[...] = (part_far[...] + part_in[0].astype(F32)).astype(BF)
    send_far.start()
    send_cot_peer.wait_recv()
    g_sum[...] = dot_nt(cot_ref[...], w_ref[:, columns(h)]) + dot_nt(
        cots[1], w_ref[:, columns(peer)]
    )
    send_part_peer.wait_recv()
    part_own[...] += part_in[1].astype(F32)

    send_cot_far.wait_recv()
    forward_cot.start()
    g_sum[...] += dot_nt(cots[0], w_ref[:, columns(far)])
    forward_cot.wait_recv()
    grad_attention = (g_sum[...] + dot_nt(cots[2], w_ref[:, columns(far_peer)])).astype(BF)
    for head in range(heads):
        mask = jnp.where(lane_head == head, 1.0, 0.0).astype(BF)
        g_stack[head * rows : (head + 1) * rows, :] = grad_attention * mask
    products = grad_attention.T.astype(F32) * attn_t[...].astype(F32)
    g_sum[:heads, :] = jnp.sum(products.reshape(heads, HD, rows), axis=1)

    def backward(head, carry):
        delta = g_sum[pl.ds(head, 1), :]
        for half, values in enumerate((v_ref, mate_v)):
            keys = slice(half * rows, (half + 1) * rows)
            grad_probs = dot_nt(values[...], g_stack[head_rows(head), :])
            grads = probs[head, keys, :] * (grad_probs - delta)
            grads_bf[keys, head_rows(head)] = grads.astype(BF)
        lanes = pl.ds(pl.multiple_of(head * HD, HD), HD)
        grads = dot(k_t[lanes, :], grads_bf[:, head_rows(head)])
        dq_t[lanes, :] = (grads * HD**-0.5).astype(BF)
        return carry

    lax.fori_loop(0, heads, backward, 0)
    dq_ref[...] = dq_t[...].T
    dv_cross[...] = dot(probs_bf[rows:, :], g_stack[...]).astype(BF)
    dk_cross[...] = dot(grads_bf[rows:, :], q_stack[...]).astype(BF)
    dv_own[...] = dot(probs_bf[:rows, :], g_stack[...])
    dk_own[...] = dot(grads_bf[:rows, :], q_stack[...])

    send_far.wait_recv()
    lo_ref[...] = (part_own[...] + far_in[...].astype(F32)).astype(BF)
    for sent in (
        send_cot_far, send_cot_peer, forward_cot, send_part_far, send_part_peer, send_far,
    ):
        sent.wait_send()


def attend(queries, key_states, value_states, mates, cotangent, out_weight, counts, partner):
    rows, width = queries.shape
    heads = width // HD
    narrow = jax.ShapeDtypeStruct((rows, width), BF)
    wide = jax.ShapeDtypeStruct((rows, width), F32)
    vmem = pl.BlockSpec(memory_space=pltpu.VMEM)
    smem = pl.BlockSpec(memory_space=pltpu.SMEM)
    scratch = [
        pltpu.VMEM((rows, width), BF),
        pltpu.VMEM((3, rows, width), BF),
        pltpu.VMEM((heads * rows, width), BF),
        pltpu.VMEM((heads * rows, width), BF),
        pltpu.VMEM((width, 2 * rows), BF),
        pltpu.VMEM((width, 2 * rows), BF),
        pltpu.VMEM((heads, 2 * rows, rows), F32),
        pltpu.VMEM((2 * rows, heads * rows), BF),
        pltpu.VMEM((2 * rows, heads * rows), BF),
        pltpu.VMEM((width, rows), BF),
        pltpu.VMEM((width, rows), BF),
        pltpu.VMEM((rows, width), F32),
        pltpu.VMEM((rows, width), F32),
        pltpu.VMEM((rows, width), F32),
        pltpu.VMEM((2, rows, width), BF),
        pltpu.VMEM((2, rows, width), BF),
        pltpu.VMEM((rows, width), BF),
        pltpu.VMEM((rows, width), BF),
        pltpu.SemaphoreType.DMA((6,)),
        pltpu.SemaphoreType.DMA((6,)),
    ]
    return pl.pallas_call(
        kernel,
        out_shape=(narrow, narrow, wide, wide, narrow, narrow),
        in_specs=[vmem] * 8 + [smem] * 2,
        out_specs=(vmem,) * 6,
        scratch_shapes=scratch,
        compiler_params=pltpu.CompilerParams(
            collective_id=0, has_side_effects=True, vmem_limit_bytes=20 << 20
        ),
        cost_estimate=pl.CostEstimate(
            flops=600_000_000, bytes_accessed=3 << 20, transcendentals=524288
        ),
    )(queries, key_states, value_states, *mates, cotangent, out_weight, counts, partner)


def finish_kernel(
    lo, dq, dk_own, dv_own, dk_direct, dk_relayed, dv_in, partner_ref,
    lo_ref, dq_ref, dk_ref, dv_ref,
):
    lo_ref[...] = lo[...]
    dq_ref[...] = dq[...]
    dk_ref[...] = (dk_own[...] + choose(partner_ref, dk_direct, dk_relayed).astype(F32)).astype(BF)
    dv_ref[...] = (dv_own[...] + dv_in[...].astype(F32)).astype(BF)


def finish(lo, dq, dk_own, dv_own, returned, partner):
    vmem = pl.BlockSpec(memory_space=pltpu.VMEM)
    smem = pl.BlockSpec(memory_space=pltpu.SMEM)
    return pl.pallas_call(
        finish_kernel,
        out_shape=(jax.ShapeDtypeStruct(lo.shape, BF),) * 4,
        in_specs=[vmem] * 7 + [smem],
        out_specs=(vmem,) * 4,
        compiler_params=pltpu.CompilerParams(vmem_limit_bytes=4 << 20),
    )(lo, dq, dk_own, dv_own, *returned, partner)


EARLY = 2
PIECES = 4


def per_device(queries, key_states, value_states, cotangent, out_weight, partner, counts):
    mates = swap_any(partner, 1, key_states, value_states)
    lo, dq, dk_own, dv_own, dk_cross, dv_cross = attend(
        queries, key_states, value_states, mates, cotangent, out_weight, counts, partner
    )
    returned = swap_any(partner, 1, dk_cross, dv_cross)
    return finish(lo, dq, dk_own, dv_own, returned, partner)


def solution(mesh):
    return jax.shard_map(
        per_device,
        mesh=mesh,
        in_specs=(
            P("seq", "head"), P("seq", "head"), P("seq", "head"), P("seq", "head"),
            P("head", None), P(), P(),
        ),
        out_specs=(P("seq", "head"),) * 4,
        check_vma=False,
    )
```

```python
import functools

import jax
import jax.numpy as jnp
from jax import lax
from jax.experimental import pallas as pl
from jax.experimental.pallas import tpu as pltpu
from jax.sharding import PartitionSpec as P

HD = 64
MESH = pl.DeviceIdType.MESH
MASKED = -1e30
BF = jnp.bfloat16
F32 = jnp.float32


def flip(index, offset):
    result = index
    for bit in range(offset.bit_length()):
        if offset >> bit & 1:
            result = result + (1 << bit) * (1 - 2 * ((index // (1 << bit)) % 2))
    return result


def dot(a, b):
    return jnp.dot(a, b, preferred_element_type=F32)


def dot_nt(a, b):
    return lax.dot_general(a, b, (((1,), (1,)), ((), ())), preferred_element_type=F32)


def remote(source, landing, send_sem, recv_sem, target):
    return pltpu.make_async_remote_copy(
        src_ref=source, dst_ref=landing, send_sem=send_sem, recv_sem=recv_sem,
        device_id=target, device_id_type=MESH,
    )


def swap_kernel(base, inputs, outputs, scratch):
    a_ref, b_ref, *c_ref, partner_ref = inputs
    a_in, a_relayed, b_in, *c_in = outputs
    (
        b_own, b_side, b_pick, partner, load_sem, a_send, a_recv, relay_send, relay_recv,
        side_send, side_recv, b_send, b_recv, c_sem,
    ) = scratch
    rows = a_ref.shape[0] // PIECES
    b, h = lax.axis_index("seq"), lax.axis_index("head")
    mate, side = (flip(b, base), h), (flip(b, 1), h)
    far = (b, (h + 2) % 4)
    targets = [side] + [mate] * bool(base) + [far] * len(c_ref)
    load_b = pltpu.make_async_copy(b_ref, b_own, load_sem.at[0])
    load_partner = pltpu.make_async_copy(partner_ref, partner, load_sem.at[1])
    if base:
        load_b.start()
        load_partner.start()
    barrier = pltpu.get_barrier_semaphore()
    for target in targets:
        pl.semaphore_signal(barrier, inc=1, device_id=target, device_id_type=MESH)
    pl.semaphore_wait(barrier, len(targets))

    def pieces(source, landing, send_sem, recv_sem, target):
        return [
            remote(
                source.at[pl.ds(i * rows, rows)], landing.at[pl.ds(i * rows, rows)],
                send_sem.at[i], recv_sem.at[i], target,
            )
            for i in range(PIECES)
        ]

    relay_a = pieces(a_in if base else a_ref, a_relayed, relay_send, relay_recv, side)
    side_b = pieces(b_ref, b_side if base else b_in, side_send, side_recv, side)
    sent_c = [remote(c_ref[0], c_in[0], c_sem.at[0], c_sem.at[1], far)] if c_ref else []
    for copy in sent_c:
        copy.start()
    for copy in side_b:
        copy.start()
    if not base:
        for copy in relay_a:
            copy.start()
        for copy in side_b + relay_a + sent_c:
            copy.wait()
        return
    direct_a = pieces(a_ref, a_in, a_send, a_recv, mate)
    picked_b = pieces(b_pick, b_in, b_send, b_recv, mate)
    for copy in direct_a:
        copy.start()
    load_b.wait()
    load_partner.wait()
    relayed = is_relayed(partner)
    for i in range(PIECES):
        side_b[i].wait_recv()
        piece = slice(i * rows, (i + 1) * rows)
        b_pick[piece, :] = jnp.where(relayed, b_side[piece, :], b_own[piece, :])
        picked_b[i].start()
    for i in range(PIECES):
        direct_a[i].wait_recv()
        relay_a[i].start()
    for copy in side_b + direct_a:
        copy.wait_send()
    for copy in picked_b + relay_a + sent_c:
        copy.wait()


def swap(base, arrays, partner):
    anywhere = pl.BlockSpec(memory_space=pl.ANY)
    shapes = [jax.ShapeDtypeStruct(x.shape, x.dtype) for x in (arrays[0], *arrays)]
    block = pltpu.VMEM(arrays[1].shape, arrays[1].dtype)
    taken, given = len(arrays) + 1, len(shapes)

    def body(*refs):
        swap_kernel(base, refs[:taken], refs[taken : taken + given], refs[taken + given :])

    return pl.pallas_call(
        body,
        out_shape=shapes,
        in_specs=[anywhere] * taken,
        out_specs=[anywhere] * given,
        scratch_shapes=[block] * 3
        + [pltpu.SMEM(partner.shape, partner.dtype), pltpu.SemaphoreType.DMA((2,))]
        + [pltpu.SemaphoreType.DMA((PIECES,))] * 8
        + [pltpu.SemaphoreType.DMA((2,))],
        compiler_params=pltpu.CompilerParams(
            collective_id=2 + base // 2, has_side_effects=True, vmem_limit_bytes=2 << 20
        ),
    )(*arrays, partner)


def swap_any(pairs, which, arrays, partner):
    branches = [
        functools.partial(lambda base, *args: swap(base, args[:-1], args[-1]), 2 * pair + pair % 2)
        for pair in pairs
    ]
    return lax.switch(which, branches, *arrays, partner)


def is_relayed(partner_ref):
    offset = partner_ref[0]
    return (offset + offset // 2) % 2 == 1


def choose(partner_ref, direct, relayed):
    return jnp.where(is_relayed(partner_ref), relayed[...], direct[...])


def kernel(inside, inputs, outputs, scratch):
    if inside:
        q_any, k_any, v_any, k_direct, k_relayed, mate_v, cot_any, w_any, counts_any, partner_any = inputs
        part_own, far_in, dq_ref, dk_own, dv_own, dk_cross, dv_cross = outputs
    else:
        (
            q_any, k_any, v_any, k_direct, k_relayed, mate_v, cot_any, w_any, counts_any, partner_any,
            cot_far,
        ) = inputs
        part_own, far_out, dq_ref, dk_own, dv_own, dk_cross, dv_cross = outputs
    (
        q_ref, k_ref, v_ref, cot_ref, w_ref, counts_ref, partner_ref, mate_k, cots, q_stack, g_stack, k_t, v_t, probs, probs_bf,
        grads_bf, attn_t, dq_t, delta, g_sum, part_far, part_out, part_in, load_sem, send_sem, recv_sem,
        *spare,
    ) = scratch
    if inside:
        cot_far, far_out = spare
    rows, width = q_ref.shape
    heads = width // HD
    b = lax.axis_index("seq")
    h = lax.axis_index("head")
    peer = h + 1 - 2 * (h % 2)
    far = (h + 2) % 4
    far_peer = 3 - h
    to_peer, to_far = (b, peer), (b, far)

    barrier = pltpu.get_barrier_semaphore()
    targets = (to_far, to_peer) if inside else (to_peer,)
    for target in targets:
        pl.semaphore_signal(barrier, inc=1, device_id=target, device_id_type=MESH)
    loads = [
        pltpu.make_async_copy(source, landing, load_sem.at[i])
        for i, (source, landing) in enumerate(
            (
                (q_any, q_ref), (partner_any, partner_ref), (counts_any, counts_ref), (k_any, k_ref),
                (v_any, v_ref), (cot_any, cot_ref), (w_any, w_ref),
            )
        )
    ]
    for load in loads:
        load.start()

    def copy(slot, source, landing, target):
        return remote(source, landing, send_sem.at[slot], recv_sem.at[slot], target)

    def columns(group):
        return pl.ds(pl.multiple_of(group * width, width), width)

    send_cot = copy(0, cot_any, cots.at[0], to_peer)
    send_cot_far = copy(1, cot_far, cots.at[1], to_peer)
    send_part_far = copy(2, part_out.at[0], part_in.at[0], to_peer)
    send_part_peer = copy(3, part_out.at[1], part_in.at[1], to_peer)
    sent = [send_cot, send_cot_far, send_part_far, send_part_peer]
    if inside:
        fetch_cot = copy(4, cot_any, cot_far, to_far)
        send_far = copy(5, far_out, far_in, to_far)
        sent += [fetch_cot, send_far]

    loads[0].wait()
    lane_head = lax.broadcasted_iota(jnp.int32, (1, width), 1) // HD
    q_scaled = q_ref[...] * jnp.asarray(HD**-0.5, BF)
    for head in range(heads):
        mask = jnp.where(lane_head == head, 1.0, 0.0).astype(BF)
        q_stack[head * rows : (head + 1) * rows, :] = q_scaled * mask
    v_t[:, rows:] = mate_v[...].T
    for load in loads[1:5]:
        load.wait()
    mate_k[...] = choose(partner_ref, k_direct, k_relayed)
    k_t[:, :rows] = k_ref[...].T
    k_t[:, rows:] = mate_k[...].T
    v_t[:, :rows] = v_ref[...].T
    key_row = lax.broadcasted_iota(jnp.int32, (rows, rows), 0)
    own_valid = key_row < counts_ref[b]
    mate_valid = key_row < counts_ref[partner_ref[b]]

    def head_rows(head):
        return pl.ds(pl.multiple_of(head * rows, rows), rows)

    def forward(head, carry):
        own = jnp.where(own_valid, dot_nt(k_ref[...], q_stack[head_rows(head), :]), MASKED)
        other = jnp.where(mate_valid, dot_nt(mate_k[...], q_stack[head_rows(head), :]), MASKED)
        top = jnp.maximum(
            jnp.max(own, axis=0, keepdims=True), jnp.max(other, axis=0, keepdims=True)
        )
        own = jnp.exp(own - top)
        other = jnp.exp(other - top)
        total = jnp.sum(own, axis=0, keepdims=True) + jnp.sum(other, axis=0, keepdims=True)
        inverse = 1.0 / total
        own = own * inverse
        other = other * inverse
        probs[head, :rows, :] = own
        probs[head, rows:, :] = other
        probs_bf[:rows, head_rows(head)] = own.astype(BF)
        probs_bf[rows:, head_rows(head)] = other.astype(BF)
        lanes = pl.ds(pl.multiple_of(head * HD, HD), HD)
        attn_t[lanes, :] = dot(v_t[lanes, :], probs_bf[:, head_rows(head)]).astype(BF)
        return carry

    if inside:
        lax.fori_loop(0, heads // 2, forward, 0, unroll=2)
        pl.semaphore_wait(barrier, 2)
        fetch_cot.start()
        send_cot.start()
        lax.fori_loop(heads // 2, heads, forward, 0, unroll=2)
    else:
        pl.semaphore_wait(barrier, 1)
        send_cot.start()
        send_cot_far.start()
        lax.fori_loop(0, heads, forward, 0, unroll=2)

    loads[6].wait()
    attention = attn_t[...].T
    part_out[0] = dot(attention, w_ref[:, columns(far_peer)]).astype(BF)
    send_part_far.start()
    part_far[...] = dot(attention, w_ref[:, columns(far)])
    part_out[1] = dot(attention, w_ref[:, columns(peer)]).astype(BF)
    send_part_peer.start()
    send_part_far.wait_recv()
    far_out[...] = (part_far[...] + part_in[0].astype(F32)).astype(BF)
    if inside:
        send_far.start()
    part_own[...] = dot(attention, w_ref[:, columns(h)])
    loads[5].wait()
    g_sum[...] = dot_nt(cot_ref[...], w_ref[:, columns(h)])
    send_cot.wait_recv()
    g_sum[...] += dot_nt(cots[0], w_ref[:, columns(peer)])
    send_part_peer.wait_recv()
    part_own[...] += part_in[1].astype(F32)

    if inside:
        fetch_cot.wait_recv()
        send_cot_far.start()
    g_sum[...] += dot_nt(cot_far[...], w_ref[:, columns(far)])
    send_cot_far.wait_recv()
    grad_attention = (g_sum[...] + dot_nt(cots[1], w_ref[:, columns(far_peer)])).astype(BF)
    for head in range(heads):
        mask = jnp.where(lane_head == head, 1.0, 0.0).astype(BF)
        g_stack[head * rows : (head + 1) * rows, :] = grad_attention * mask
    products = grad_attention.T.astype(F32) * attn_t[...].astype(F32)
    delta[...] = jnp.sum(products.reshape(heads, HD, rows), axis=1)

    def backward(head, carry):
        row_delta = delta[pl.ds(head, 1), :]
        for half, values in enumerate((v_ref, mate_v)):
            keys = slice(half * rows, (half + 1) * rows)
            grad_probs = dot_nt(values[...], g_stack[head_rows(head), :])
            grads = probs[head, keys, :] * (grad_probs - row_delta)
            grads_bf[keys, head_rows(head)] = grads.astype(BF)
        lanes = pl.ds(pl.multiple_of(head * HD, HD), HD)
        grads = dot(k_t[lanes, :], grads_bf[:, head_rows(head)])
        dq_t[lanes, :] = (grads * HD**-0.5).astype(BF)
        return carry

    lax.fori_loop(0, heads, backward, 0, unroll=2)
    dq_ref[...] = dq_t[...].T
    dv_cross[...] = dot(probs_bf[rows:, :], g_stack[...]).astype(BF)
    dk_cross[...] = dot(grads_bf[rows:, :], q_stack[...]).astype(BF)
    dv_own[...] = dot(probs_bf[:rows, :], g_stack[...])
    dk_own[...] = dot(grads_bf[:rows, :], q_stack[...])
    if inside:
        send_far.wait_recv()
    for done in sent:
        done.wait_send()


def attend(inside, *operands):
    queries, counts, partner = operands[0], operands[8], operands[9]
    rows, width = queries.shape
    heads = width // HD
    narrow = jax.ShapeDtypeStruct((rows, width), BF)
    wide = jax.ShapeDtypeStruct((rows, width), F32)
    vmem = pl.BlockSpec(memory_space=pltpu.VMEM)
    anywhere = pl.BlockSpec(memory_space=pl.ANY)
    block = pltpu.VMEM((rows, width), BF)
    scratch = [
        block,
        block,
        block,
        block,
        pltpu.VMEM(operands[7].shape, BF),
        pltpu.SMEM(counts.shape, counts.dtype),
        pltpu.SMEM(partner.shape, partner.dtype),
        block,
        pltpu.VMEM((2, rows, width), BF),
        pltpu.VMEM((heads * rows, width), BF),
        pltpu.VMEM((heads * rows, width), BF),
        pltpu.VMEM((width, 2 * rows), BF),
        pltpu.VMEM((width, 2 * rows), BF),
        pltpu.VMEM((heads, 2 * rows, rows), F32),
        pltpu.VMEM((2 * rows, heads * rows), BF),
        pltpu.VMEM((2 * rows, heads * rows), BF),
        pltpu.VMEM((width, rows), BF),
        pltpu.VMEM((width, rows), BF),
        pltpu.VMEM((heads, rows), F32),
        pltpu.VMEM((rows, width), F32),
        pltpu.VMEM((rows, width), F32),
        pltpu.VMEM((2, rows, width), BF),
        pltpu.VMEM((2, rows, width), BF),
        pltpu.SemaphoreType.DMA((7,)),
        pltpu.SemaphoreType.DMA((6,)),
        pltpu.SemaphoreType.DMA((6,)),
    ] + [block] * (2 * inside)
    in_specs = [anywhere] * 3 + [vmem] * 3 + [anywhere] * 4 + [vmem] * (not inside)
    taken, given = len(in_specs), 7

    def body(*refs):
        kernel(inside, refs[:taken], refs[taken : taken + given], refs[taken + given :])

    return pl.pallas_call(
        body,
        out_shape=(wide, narrow, narrow, wide, wide, narrow, narrow),
        in_specs=in_specs,
        out_specs=(vmem,) * given,
        scratch_shapes=scratch,
        compiler_params=pltpu.CompilerParams(
            collective_id=int(inside), has_side_effects=True, vmem_limit_bytes=20 << 20
        ),
        cost_estimate=pl.CostEstimate(
            flops=600_000_000, bytes_accessed=3 << 20, transcendentals=524288
        ),
    )(*operands)


def finish_kernel(
    part_own, far_in, dq, dk_own, dv_own, dk_direct, dk_relayed, dv_in, partner_any,
    lo_out, dq_out, dk_out, dv_out, lo, dk, dv, partner, sems,
):
    load = pltpu.make_async_copy(partner_any, partner, sems.at[0])
    load.start()
    stores = [
        pltpu.make_async_copy(source, target, sems.at[1 + i])
        for i, (source, target) in enumerate(((dq, dq_out), (lo, lo_out), (dv, dv_out), (dk, dk_out)))
    ]
    stores[0].start()
    lo[...] = (part_own[...] + far_in[...].astype(F32)).astype(BF)
    stores[1].start()
    dv[...] = (dv_own[...] + dv_in[...].astype(F32)).astype(BF)
    stores[2].start()
    load.wait()
    dk[...] = (dk_own[...] + choose(partner, dk_direct, dk_relayed).astype(F32)).astype(BF)
    stores[3].start()
    for store in stores:
        store.wait()


def finish(part_own, far_in, dq, dk_own, dv_own, returned, partner):
    vmem = pl.BlockSpec(memory_space=pltpu.VMEM)
    anywhere = pl.BlockSpec(memory_space=pl.ANY)
    return pl.pallas_call(
        finish_kernel,
        out_shape=(jax.ShapeDtypeStruct(dq.shape, BF),) * 4,
        in_specs=[vmem] * 8 + [anywhere],
        out_specs=(anywhere,) * 4,
        scratch_shapes=[pltpu.VMEM(dq.shape, BF)] * 3
        + [pltpu.SMEM(partner.shape, partner.dtype), pltpu.SemaphoreType.DMA((5,))],
        compiler_params=pltpu.CompilerParams(vmem_limit_bytes=4 << 20),
    )(part_own, far_in, dq, dk_own, dv_own, *returned, partner)


PIECES = 4


def near(pair):
    return pair // 2 % 4 == 0


def per_device(queries, key_states, value_states, cotangent, out_weight, partner, counts):
    pair = partner[0] // 2
    everything = range(partner.shape[0] // 2)
    near_pairs = [p for p in everything if near(p)]
    long_pairs = [p for p in everything if not near(p)]

    def stay(queries, key_states, value_states, cotangent, out_weight, partner, counts):
        which = pair // 8 * 2 + pair % 2
        *mates, cotangent_far = swap_any(
            near_pairs, which, (key_states, value_states, cotangent), partner
        )
        part_own, far_out, dq, dk_own, dv_own, dk_cross, dv_cross = attend(
            False, queries, key_states, value_states, *mates, cotangent, out_weight, counts,
            partner, cotangent_far,
        )
        *returned, far_in = swap_any(near_pairs, which, (dk_cross, dv_cross, far_out), partner)
        return finish(part_own, far_in, dq, dk_own, dv_own, returned, partner)

    def cross(queries, key_states, value_states, cotangent, out_weight, partner, counts):
        which = (pair // 8 * 3 + pair // 2 % 4 - 1) * 2 + pair % 2
        mates = swap_any(long_pairs, which, (key_states, value_states), partner)
        part_own, far_in, dq, dk_own, dv_own, dk_cross, dv_cross = attend(
            True, queries, key_states, value_states, *mates, cotangent, out_weight, counts, partner
        )
        returned = swap_any(long_pairs, which, (dk_cross, dv_cross), partner)
        return finish(part_own, far_in, dq, dk_own, dv_own, returned, partner)

    operands = queries, key_states, value_states, cotangent, out_weight, partner, counts
    if not long_pairs:
        return stay(*operands)
    return lax.cond(near(pair), stay, cross, *operands)


def solution(mesh):
    return jax.shard_map(
        per_device,
        mesh=mesh,
        in_specs=(
            P("seq", "head"), P("seq", "head"), P("seq", "head"), P("seq", "head"),
            P("head", None), P(), P(),
        ),
        out_specs=(P("seq", "head"),) * 4,
        check_vma=False,
    )
```

```python
import functools

import jax
import jax.numpy as jnp
from jax import lax
from jax.experimental import pallas as pl
from jax.experimental.pallas import tpu as pltpu
from jax.sharding import PartitionSpec as P

HD = 64
MESH = pl.DeviceIdType.MESH
MASKED = -1e30
BF = jnp.bfloat16
F32 = jnp.float32


def flip(index, offset):
    result = index
    for bit in range(offset.bit_length()):
        if offset >> bit & 1:
            result = result + (1 << bit) * (1 - 2 * ((index // (1 << bit)) % 2))
    return result


def dot(a, b):
    return jnp.dot(a, b, preferred_element_type=F32)


def dot_nt(a, b):
    return lax.dot_general(a, b, (((1,), (1,)), ((), ())), preferred_element_type=F32)


def remote(source, landing, send_sem, recv_sem, target):
    return pltpu.make_async_remote_copy(
        src_ref=source, dst_ref=landing, send_sem=send_sem, recv_sem=recv_sem,
        device_id=target, device_id_type=MESH,
    )


def swap_kernel(base, inputs, outputs, scratch):
    a_ref, b_ref, *c_ref, partner_ref = inputs
    a_in, a_relayed, b_in, *c_in = outputs
    (
        b_own, b_side, b_pick, partner, load_sem, a_send, a_recv, relay_send, relay_recv,
        side_send, side_recv, b_send, b_recv, c_sem,
    ) = scratch
    rows = a_ref.shape[0] // PIECES
    b, h = lax.axis_index("seq"), lax.axis_index("head")
    mate, side = (flip(b, base), h), (flip(b, 1), h)
    far = (b, (h + 2) % 4)
    targets = [side] + [mate] * bool(base) + [far] * len(c_ref)
    load_b = pltpu.make_async_copy(b_ref, b_own, load_sem.at[0])
    load_partner = pltpu.make_async_copy(partner_ref, partner, load_sem.at[1])
    if base:
        load_b.start()
        load_partner.start()
    barrier = pltpu.get_barrier_semaphore()
    for target in targets:
        pl.semaphore_signal(barrier, inc=1, device_id=target, device_id_type=MESH)
    pl.semaphore_wait(barrier, len(targets))

    def pieces(source, landing, send_sem, recv_sem, target):
        return [
            remote(
                source.at[pl.ds(i * rows, rows)], landing.at[pl.ds(i * rows, rows)],
                send_sem.at[i], recv_sem.at[i], target,
            )
            for i in range(PIECES)
        ]

    relay_a = pieces(a_in if base else a_ref, a_relayed, relay_send, relay_recv, side)
    side_b = pieces(b_ref, b_side if base else b_in, side_send, side_recv, side)
    sent_c = [remote(c_ref[0], c_in[0], c_sem.at[0], c_sem.at[1], far)] if c_ref else []
    for copy in sent_c:
        copy.start()
    if not base:
        for copy in side_b + relay_a:
            copy.start()
        for copy in side_b + relay_a + sent_c:
            copy.wait()
        return
    direct_a = pieces(a_ref, a_in, a_send, a_recv, mate)
    picked_b = pieces(b_pick, b_in, b_send, b_recv, mate)
    for copy in direct_a + side_b:
        copy.start()
    load_b.wait()
    load_partner.wait()
    relayed = is_relayed(partner)
    for i in range(PIECES):
        side_b[i].wait_recv()
        piece = slice(i * rows, (i + 1) * rows)
        b_pick[piece, :] = jnp.where(relayed, b_side[piece, :], b_own[piece, :])
        picked_b[i].start()
    for i in range(PIECES):
        direct_a[i].wait_recv()
        relay_a[i].start()
    for copy in side_b + direct_a:
        copy.wait_send()
    for copy in picked_b + relay_a + sent_c:
        copy.wait()


def swap(base, arrays, partner):
    anywhere = pl.BlockSpec(memory_space=pl.ANY)
    shapes = [jax.ShapeDtypeStruct(x.shape, x.dtype) for x in (arrays[0], *arrays)]
    block = pltpu.VMEM(arrays[1].shape, arrays[1].dtype)
    taken, given = len(arrays) + 1, len(shapes)

    def body(*refs):
        swap_kernel(base, refs[:taken], refs[taken : taken + given], refs[taken + given :])

    return pl.pallas_call(
        body,
        out_shape=shapes,
        in_specs=[anywhere] * taken,
        out_specs=[anywhere] * given,
        scratch_shapes=[block] * 3
        + [pltpu.SMEM(partner.shape, partner.dtype), pltpu.SemaphoreType.DMA((2,))]
        + [pltpu.SemaphoreType.DMA((PIECES,))] * 8
        + [pltpu.SemaphoreType.DMA((2,))],
        compiler_params=pltpu.CompilerParams(
            collective_id=2 + base // 2, has_side_effects=True, vmem_limit_bytes=2 << 20
        ),
    )(*arrays, partner)


def swap_any(pairs, which, arrays, partner):
    branches = [
        functools.partial(lambda base, *args: swap(base, args[:-1], args[-1]), 2 * pair + pair % 2)
        for pair in pairs
    ]
    return lax.switch(which, branches, *arrays, partner)


def is_relayed(partner_ref):
    offset = partner_ref[0] % partner_ref.shape[0]
    return (offset + offset // 2) % 2 == 1


def choose(partner_ref, direct, relayed):
    return jnp.where(is_relayed(partner_ref), relayed[...], direct[...])


def kernel(inside, inputs, outputs, scratch):
    if inside:
        q_any, k_any, v_any, k_direct, k_relayed, mate_v, cot_any, w_any, partner_any = inputs
        part_own, far_in, dq_ref, dk_own, dv_own, dk_cross, dv_cross = outputs
    else:
        (
            q_any, k_any, v_any, k_direct, k_relayed, mate_v, cot_any, w_any, partner_any,
            cot_far,
        ) = inputs
        part_own, far_out, dq_ref, dk_own, dv_own, dk_cross, dv_cross = outputs
    (
        q_ref, k_ref, v_ref, cot_ref, w_ref, partner_ref, mate_k, cots, q_stack, g_stack, k_t, v_t, probs, probs_bf,
        grads_bf, attn_t, dq_t, delta, g_sum, part_far, part_out, part_in, load_sem, send_sem, recv_sem,
        *spare,
    ) = scratch
    if inside:
        cot_far, far_out = spare
    rows, width = q_ref.shape
    heads = width // HD
    b = lax.axis_index("seq")
    h = lax.axis_index("head")
    peer = h + 1 - 2 * (h % 2)
    far = (h + 2) % 4
    far_peer = 3 - h
    to_peer, to_far = (b, peer), (b, far)

    barrier = pltpu.get_barrier_semaphore()
    targets = (to_far, to_peer) if inside else (to_peer,)
    for target in targets:
        pl.semaphore_signal(barrier, inc=1, device_id=target, device_id_type=MESH)
    loads = [
        pltpu.make_async_copy(source, landing, load_sem.at[i])
        for i, (source, landing) in enumerate(
            (
                (q_any, q_ref), (partner_any, partner_ref), (k_any, k_ref), (v_any, v_ref),
                (cot_any, cot_ref), (w_any, w_ref),
            )
        )
    ]
    for load in loads:
        load.start()

    def copy(slot, source, landing, target):
        return remote(source, landing, send_sem.at[slot], recv_sem.at[slot], target)

    def columns(group):
        return pl.ds(pl.multiple_of(group * width, width), width)

    send_cot = copy(0, cot_any, cots.at[0], to_peer)
    send_cot_far = copy(1, cot_far, cots.at[1], to_peer)
    send_part_far = copy(2, part_out.at[0], part_in.at[0], to_peer)
    send_part_peer = copy(3, part_out.at[1], part_in.at[1], to_peer)
    sent = [send_cot, send_cot_far, send_part_far, send_part_peer]
    if inside:
        fetch_cot = copy(4, cot_any, cot_far, to_far)
        send_far = copy(5, far_out, far_in, to_far)
        sent += [fetch_cot, send_far]

    loads[0].wait()
    lane_head = lax.broadcasted_iota(jnp.int32, (1, width), 1) // HD
    q_scaled = q_ref[...] * jnp.asarray(HD**-0.5, BF)
    for head in range(heads):
        mask = jnp.where(lane_head == head, 1.0, 0.0).astype(BF)
        q_stack[head * rows : (head + 1) * rows, :] = q_scaled * mask
    v_t[:, rows:] = mate_v[...].T
    for load in loads[1:4]:
        load.wait()
    mate_k[...] = choose(partner_ref, k_direct, k_relayed)
    k_t[:, :rows] = k_ref[...].T
    k_t[:, rows:] = mate_k[...].T
    v_t[:, :rows] = v_ref[...].T
    key_row = lax.broadcasted_iota(jnp.int32, (rows, rows), 0)
    blocks = partner_ref.shape[0]
    own_valid = key_row < partner_ref[b] // blocks
    mate_valid = key_row < partner_ref[partner_ref[b] % blocks] // blocks

    def head_rows(head):
        return pl.ds(pl.multiple_of(head * rows, rows), rows)

    def forward(head, carry):
        own = jnp.where(own_valid, dot_nt(k_ref[...], q_stack[head_rows(head), :]), MASKED)
        other = jnp.where(mate_valid, dot_nt(mate_k[...], q_stack[head_rows(head), :]), MASKED)
        top = jnp.maximum(
            jnp.max(own, axis=0, keepdims=True), jnp.max(other, axis=0, keepdims=True)
        )
        own = jnp.exp(own - top)
        other = jnp.exp(other - top)
        total = jnp.sum(own, axis=0, keepdims=True) + jnp.sum(other, axis=0, keepdims=True)
        inverse = 1.0 / total
        own = own * inverse
        other = other * inverse
        probs[head, :rows, :] = own
        probs[head, rows:, :] = other
        probs_bf[:rows, head_rows(head)] = own.astype(BF)
        probs_bf[rows:, head_rows(head)] = other.astype(BF)
        lanes = pl.ds(pl.multiple_of(head * HD, HD), HD)
        attn_t[lanes, :] = dot(v_t[lanes, :], probs_bf[:, head_rows(head)]).astype(BF)
        return carry

    if inside:
        lax.fori_loop(0, heads // 2, forward, 0, unroll=2)
        pl.semaphore_wait(barrier, 2)
        fetch_cot.start()
        send_cot.start()
        lax.fori_loop(heads // 2, heads, forward, 0, unroll=2)
    else:
        pl.semaphore_wait(barrier, 1)
        send_cot.start()
        send_cot_far.start()
        lax.fori_loop(0, heads, forward, 0, unroll=2)

    loads[5].wait()
    attention = attn_t[...].T
    part_out[0] = dot(attention, w_ref[:, columns(far_peer)]).astype(BF)
    send_part_far.start()
    part_far[...] = dot(attention, w_ref[:, columns(far)])
    part_out[1] = dot(attention, w_ref[:, columns(peer)]).astype(BF)
    send_part_peer.start()
    send_part_far.wait_recv()
    far_out[...] = (part_far[...] + part_in[0].astype(F32)).astype(BF)
    if inside:
        send_far.start()
    part_own[...] = dot(attention, w_ref[:, columns(h)])
    loads[4].wait()
    g_sum[...] = dot_nt(cot_ref[...], w_ref[:, columns(h)])
    send_cot.wait_recv()
    g_sum[...] += dot_nt(cots[0], w_ref[:, columns(peer)])
    send_part_peer.wait_recv()
    part_own[...] += part_in[1].astype(F32)

    if inside:
        fetch_cot.wait_recv()
        send_cot_far.start()
    g_sum[...] += dot_nt(cot_far[...], w_ref[:, columns(far)])
    send_cot_far.wait_recv()
    grad_attention = (g_sum[...] + dot_nt(cots[1], w_ref[:, columns(far_peer)])).astype(BF)
    for head in range(heads):
        mask = jnp.where(lane_head == head, 1.0, 0.0).astype(BF)
        g_stack[head * rows : (head + 1) * rows, :] = grad_attention * mask
    products = grad_attention.T.astype(F32) * attn_t[...].astype(F32)
    delta[...] = jnp.sum(products.reshape(heads, HD, rows), axis=1)

    def backward(head, carry):
        row_delta = delta[pl.ds(head, 1), :]
        for half, values in enumerate((v_ref, mate_v)):
            keys = slice(half * rows, (half + 1) * rows)
            grad_probs = dot_nt(values[...], g_stack[head_rows(head), :])
            grads = probs[head, keys, :] * (grad_probs - row_delta)
            grads_bf[keys, head_rows(head)] = grads.astype(BF)
        lanes = pl.ds(pl.multiple_of(head * HD, HD), HD)
        grads = dot(k_t[lanes, :], grads_bf[:, head_rows(head)])
        dq_t[lanes, :] = (grads * HD**-0.5).astype(BF)
        return carry

    lax.fori_loop(0, heads, backward, 0, unroll=2)
    dq_ref[...] = dq_t[...].T
    dv_cross[...] = dot(probs_bf[rows:, :], g_stack[...]).astype(BF)
    dk_cross[...] = dot(grads_bf[rows:, :], q_stack[...]).astype(BF)
    dv_own[...] = dot(probs_bf[:rows, :], g_stack[...])
    dk_own[...] = dot(grads_bf[:rows, :], q_stack[...])
    if inside:
        send_far.wait_recv()
    for done in sent:
        done.wait_send()


def attend(inside, *operands):
    queries, partner = operands[0], operands[8]
    rows, width = queries.shape
    heads = width // HD
    narrow = jax.ShapeDtypeStruct((rows, width), BF)
    wide = jax.ShapeDtypeStruct((rows, width), F32)
    vmem = pl.BlockSpec(memory_space=pltpu.VMEM)
    anywhere = pl.BlockSpec(memory_space=pl.ANY)
    block = pltpu.VMEM((rows, width), BF)
    scratch = [
        block,
        block,
        block,
        block,
        pltpu.VMEM(operands[7].shape, BF),
        pltpu.SMEM(partner.shape, partner.dtype),
        block,
        pltpu.VMEM((2, rows, width), BF),
        pltpu.VMEM((heads * rows, width), BF),
        pltpu.VMEM((heads * rows, width), BF),
        pltpu.VMEM((width, 2 * rows), BF),
        pltpu.VMEM((width, 2 * rows), BF),
        pltpu.VMEM((heads, 2 * rows, rows), F32),
        pltpu.VMEM((2 * rows, heads * rows), BF),
        pltpu.VMEM((2 * rows, heads * rows), BF),
        pltpu.VMEM((width, rows), BF),
        pltpu.VMEM((width, rows), BF),
        pltpu.VMEM((heads, rows), F32),
        pltpu.VMEM((rows, width), F32),
        pltpu.VMEM((rows, width), F32),
        pltpu.VMEM((2, rows, width), BF),
        pltpu.VMEM((2, rows, width), BF),
        pltpu.SemaphoreType.DMA((6,)),
        pltpu.SemaphoreType.DMA((6,)),
        pltpu.SemaphoreType.DMA((6,)),
    ] + [block] * (2 * inside)
    in_specs = [anywhere] * 3 + [vmem] * 3 + [anywhere] * 3 + [vmem] * (not inside)
    taken, given = len(in_specs), 7

    def body(*refs):
        kernel(inside, refs[:taken], refs[taken : taken + given], refs[taken + given :])

    return pl.pallas_call(
        body,
        out_shape=(wide, narrow, narrow, wide, wide, narrow, narrow),
        in_specs=in_specs,
        out_specs=(vmem,) * given,
        scratch_shapes=scratch,
        compiler_params=pltpu.CompilerParams(
            collective_id=int(inside), has_side_effects=True, vmem_limit_bytes=20 << 20
        ),
        cost_estimate=pl.CostEstimate(
            flops=600_000_000, bytes_accessed=3 << 20, transcendentals=524288
        ),
    )(*operands)


def finish_kernel(
    part_own, far_in, dq, dk_own, dv_own, dk_direct, dk_relayed, dv_in, partner_any,
    lo_out, dq_out, dk_out, dv_out, lo, dk, dv, partner, sems,
):
    load = pltpu.make_async_copy(partner_any, partner, sems.at[0])
    load.start()
    stores = [
        pltpu.make_async_copy(source, target, sems.at[1 + i])
        for i, (source, target) in enumerate(((dq, dq_out), (lo, lo_out), (dv, dv_out), (dk, dk_out)))
    ]
    stores[0].start()
    lo[...] = (part_own[...] + far_in[...].astype(F32)).astype(BF)
    stores[1].start()
    dv[...] = (dv_own[...] + dv_in[...].astype(F32)).astype(BF)
    stores[2].start()
    load.wait()
    dk[...] = (dk_own[...] + choose(partner, dk_direct, dk_relayed).astype(F32)).astype(BF)
    stores[3].start()
    for store in stores:
        store.wait()


def finish(part_own, far_in, dq, dk_own, dv_own, returned, partner):
    vmem = pl.BlockSpec(memory_space=pltpu.VMEM)
    anywhere = pl.BlockSpec(memory_space=pl.ANY)
    return pl.pallas_call(
        finish_kernel,
        out_shape=(jax.ShapeDtypeStruct(dq.shape, BF),) * 4,
        in_specs=[vmem] * 8 + [anywhere],
        out_specs=(anywhere,) * 4,
        scratch_shapes=[pltpu.VMEM(dq.shape, BF)] * 3
        + [pltpu.SMEM(partner.shape, partner.dtype), pltpu.SemaphoreType.DMA((5,))],
        compiler_params=pltpu.CompilerParams(vmem_limit_bytes=4 << 20),
    )(part_own, far_in, dq, dk_own, dv_own, *returned, partner)


PIECES = 2


def near(pair):
    return pair // 2 % 4 == 0


def per_device(queries, key_states, value_states, cotangent, out_weight, partner, counts):
    blocks = partner.shape[0]
    partner = partner + blocks * counts
    pair = partner[0] % blocks // 2
    everything = range(partner.shape[0] // 2)
    near_pairs = [p for p in everything if near(p)]
    long_pairs = [p for p in everything if not near(p)]

    def stay(queries, key_states, value_states, cotangent, out_weight, partner):
        which = pair // 8 * 2 + pair % 2
        *mates, cotangent_far = swap_any(
            near_pairs, which, (key_states, value_states, cotangent), partner
        )
        part_own, far_out, dq, dk_own, dv_own, dk_cross, dv_cross = attend(
            False, queries, key_states, value_states, *mates, cotangent, out_weight, partner,
            cotangent_far,
        )
        *returned, far_in = swap_any(near_pairs, which, (dk_cross, dv_cross, far_out), partner)
        return finish(part_own, far_in, dq, dk_own, dv_own, returned, partner)

    def cross(queries, key_states, value_states, cotangent, out_weight, partner):
        which = (pair // 8 * 3 + pair // 2 % 4 - 1) * 2 + pair % 2
        mates = swap_any(long_pairs, which, (key_states, value_states), partner)
        part_own, far_in, dq, dk_own, dv_own, dk_cross, dv_cross = attend(
            True, queries, key_states, value_states, *mates, cotangent, out_weight, partner
        )
        returned = swap_any(long_pairs, which, (dk_cross, dv_cross), partner)
        return finish(part_own, far_in, dq, dk_own, dv_own, returned, partner)

    operands = queries, key_states, value_states, cotangent, out_weight, partner
    if not long_pairs:
        return stay(*operands)
    return lax.cond(near(pair), stay, cross, *operands)


def solution(mesh):
    return jax.shard_map(
        per_device,
        mesh=mesh,
        in_specs=(
            P("seq", "head"), P("seq", "head"), P("seq", "head"), P("seq", "head"),
            P("head", None), P(), P(),
        ),
        out_specs=(P("seq", "head"),) * 4,
        check_vma=False,
    )
```

```python
import functools

import jax
import jax.numpy as jnp
from jax import lax
from jax.experimental import pallas as pl
from jax.experimental.pallas import tpu as pltpu
from jax.sharding import PartitionSpec as P

HD = 64
MESH = pl.DeviceIdType.MESH
MASKED = -1e30
BF = jnp.bfloat16
F32 = jnp.float32


def flip(index, offset):
    result = index
    for bit in range(offset.bit_length()):
        if offset >> bit & 1:
            result = result + (1 << bit) * (1 - 2 * ((index // (1 << bit)) % 2))
    return result


def dot(a, b):
    return jnp.dot(a, b, preferred_element_type=F32)


def dot_nt(a, b):
    return lax.dot_general(a, b, (((1,), (1,)), ((), ())), preferred_element_type=F32)


def remote(source, landing, send_sem, recv_sem, target):
    return pltpu.make_async_remote_copy(
        src_ref=source, dst_ref=landing, send_sem=send_sem, recv_sem=recv_sem,
        device_id=target, device_id_type=MESH,
    )


def swap_kernel(base, inputs, outputs, scratch):
    a_ref, b_ref, *c_ref, partner_ref = inputs
    a_in, a_relayed, b_in, *c_in = outputs
    (
        b_own, b_side, b_pick, partner, load_sem, a_send, a_recv, relay_send, relay_recv,
        side_send, side_recv, b_send, b_recv, c_sem,
    ) = scratch
    rows = a_ref.shape[0] // PIECES
    b, h = lax.axis_index("seq"), lax.axis_index("head")
    mate, side = (flip(b, base), h), (flip(b, 1), h)
    far = (b, (h + 2) % 4)
    targets = [side] + [mate] * bool(base) + [far] * len(c_ref)
    load_b = pltpu.make_async_copy(b_ref, b_own, load_sem.at[0])
    load_partner = pltpu.make_async_copy(partner_ref, partner, load_sem.at[1])
    if base:
        load_b.start()
        load_partner.start()
    barrier = pltpu.get_barrier_semaphore()
    for target in targets:
        pl.semaphore_signal(barrier, inc=1, device_id=target, device_id_type=MESH)
    pl.semaphore_wait(barrier, len(targets))

    def pieces(source, landing, send_sem, recv_sem, target):
        return [
            remote(
                source.at[pl.ds(i * rows, rows)], landing.at[pl.ds(i * rows, rows)],
                send_sem.at[i], recv_sem.at[i], target,
            )
            for i in range(PIECES)
        ]

    relay_a = pieces(a_in if base else a_ref, a_relayed, relay_send, relay_recv, side)
    side_b = pieces(b_ref, b_side if base else b_in, side_send, side_recv, side)
    sent_c = [remote(c_ref[0], c_in[0], c_sem.at[0], c_sem.at[1], far)] if c_ref else []
    for copy in sent_c:
        copy.start()
    if not base:
        for copy in side_b + relay_a:
            copy.start()
        for copy in side_b + relay_a + sent_c:
            copy.wait()
        return
    direct_a = pieces(a_ref, a_in, a_send, a_recv, mate)
    picked_b = pieces(b_pick, b_in, b_send, b_recv, mate)
    for copy in direct_a + side_b:
        copy.start()
    load_b.wait()
    load_partner.wait()
    relayed = is_relayed(partner)
    for i in range(PIECES):
        side_b[i].wait_recv()
        piece = slice(i * rows, (i + 1) * rows)
        b_pick[piece, :] = jnp.where(relayed, b_side[piece, :], b_own[piece, :])
        picked_b[i].start()
    for i in range(PIECES):
        direct_a[i].wait_recv()
        relay_a[i].start()
    for copy in side_b + direct_a:
        copy.wait_send()
    for copy in picked_b + relay_a + sent_c:
        copy.wait()


def swap(base, arrays, partner):
    anywhere = pl.BlockSpec(memory_space=pl.ANY)
    shapes = [jax.ShapeDtypeStruct(x.shape, x.dtype) for x in (arrays[0], *arrays)]
    block = pltpu.VMEM(arrays[1].shape, arrays[1].dtype)
    taken, given = len(arrays) + 1, len(shapes)

    def body(*refs):
        swap_kernel(base, refs[:taken], refs[taken : taken + given], refs[taken + given :])

    return pl.pallas_call(
        body,
        out_shape=shapes,
        in_specs=[anywhere] * taken,
        out_specs=[anywhere] * given,
        scratch_shapes=[block] * 3
        + [pltpu.SMEM(partner.shape, partner.dtype), pltpu.SemaphoreType.DMA((2,))]
        + [pltpu.SemaphoreType.DMA((PIECES,))] * 8
        + [pltpu.SemaphoreType.DMA((2,))],
        compiler_params=pltpu.CompilerParams(
            collective_id=2 + base // 2, has_side_effects=True, vmem_limit_bytes=2 << 20
        ),
    )(*arrays, partner)


def swap_any(pairs, which, arrays, partner):
    branches = [
        functools.partial(lambda base, *args: swap(base, args[:-1], args[-1]), 2 * pair + pair % 2)
        for pair in pairs
    ]
    return lax.switch(which, branches, *arrays, partner)


def is_relayed(partner_ref):
    offset = partner_ref[0] % partner_ref.shape[0]
    return (offset + offset // 2) % 2 == 1


def choose(partner_ref, direct, relayed):
    return jnp.where(is_relayed(partner_ref), relayed[...], direct[...])


def kernel(inside, inputs, outputs, scratch):
    if inside:
        q_any, k_any, v_any, k_direct, k_relayed, mate_v, cot_any, w_any, partner_any = inputs
        part_own, far_in, dq_ref, dk_own, dv_own, dk_cross, dv_cross = outputs
    else:
        (
            q_any, k_any, v_any, k_direct, k_relayed, mate_v, cot_any, w_any, partner_any,
            cot_far,
        ) = inputs
        part_own, far_out, dq_ref, dk_own, dv_own, dk_cross, dv_cross = outputs
    (
        q_ref, k_ref, v_ref, cot_ref, w_ref, partner_ref, mate_k, cots, q_stack, g_stack, k_t, v_t, probs, probs_bf,
        grads_bf, attn_t, dq_t, delta, g_sum, part_far, part_out, part_in, load_sem, send_sem, recv_sem,
        *spare,
    ) = scratch
    if inside:
        cot_far, far_out = spare
    rows, width = q_ref.shape
    heads = width // HD
    b = lax.axis_index("seq")
    h = lax.axis_index("head")
    peer = h + 1 - 2 * (h % 2)
    far = (h + 2) % 4
    far_peer = 3 - h
    to_peer, to_far = (b, peer), (b, far)

    barrier = pltpu.get_barrier_semaphore()
    targets = (to_far, to_peer) if inside else (to_peer,)
    for target in targets:
        pl.semaphore_signal(barrier, inc=1, device_id=target, device_id_type=MESH)
    loads = [
        pltpu.make_async_copy(source, landing, load_sem.at[i])
        for i, (source, landing) in enumerate(
            (
                (q_any, q_ref), (partner_any, partner_ref), (k_any, k_ref), (v_any, v_ref),
                (cot_any, cot_ref), (w_any, w_ref),
            )
        )
    ]
    for load in loads:
        load.start()

    def copy(slot, source, landing, target):
        return remote(source, landing, send_sem.at[slot], recv_sem.at[slot], target)

    def columns(group):
        return pl.ds(pl.multiple_of(group * width, width), width)

    send_cot = copy(0, cot_any, cots.at[0], to_peer)
    send_cot_far = copy(1, cot_far, cots.at[1], to_peer)
    send_part_far = copy(2, part_out.at[0], part_in.at[0], to_peer)
    send_part_peer = copy(3, part_out.at[1], part_in.at[1], to_peer)
    sent = [send_cot, send_cot_far, send_part_far, send_part_peer]
    if inside:
        fetch_cot = copy(4, cot_any, cot_far, to_far)
        send_far = copy(5, far_out, far_in, to_far)
        sent += [fetch_cot, send_far]

    loads[0].wait()
    lane_head = lax.broadcasted_iota(jnp.int32, (1, width), 1) // HD
    q_scaled = q_ref[...] * jnp.asarray(HD**-0.5, BF)
    for head in range(heads):
        mask = jnp.where(lane_head == head, 1.0, 0.0).astype(BF)
        q_stack[head * rows : (head + 1) * rows, :] = q_scaled * mask
    v_t[:, rows:] = mate_v[...].T
    for load in loads[1:4]:
        load.wait()
    mate_k[...] = choose(partner_ref, k_direct, k_relayed)
    k_t[:, :rows] = k_ref[...].T
    k_t[:, rows:] = mate_k[...].T
    v_t[:, :rows] = v_ref[...].T
    key_row = lax.broadcasted_iota(jnp.int32, (rows, rows), 0)
    blocks = partner_ref.shape[0]
    own_valid = key_row < partner_ref[b] // blocks
    mate_valid = key_row < partner_ref[partner_ref[b] % blocks] // blocks

    def head_rows(head):
        return pl.ds(pl.multiple_of(head * rows, rows), rows)

    def forward(head, carry):
        own = jnp.where(own_valid, dot_nt(k_ref[...], q_stack[head_rows(head), :]), MASKED)
        other = jnp.where(mate_valid, dot_nt(mate_k[...], q_stack[head_rows(head), :]), MASKED)
        top = jnp.maximum(
            jnp.max(own, axis=0, keepdims=True), jnp.max(other, axis=0, keepdims=True)
        )
        own = jnp.exp(own - top)
        other = jnp.exp(other - top)
        total = jnp.sum(own, axis=0, keepdims=True) + jnp.sum(other, axis=0, keepdims=True)
        inverse = 1.0 / total
        own = own * inverse
        other = other * inverse
        probs[head, :rows, :] = own
        probs[head, rows:, :] = other
        probs_bf[:rows, head_rows(head)] = own.astype(BF)
        probs_bf[rows:, head_rows(head)] = other.astype(BF)
        lanes = pl.ds(pl.multiple_of(head * HD, HD), HD)
        attn_t[lanes, :] = dot(v_t[lanes, :], probs_bf[:, head_rows(head)]).astype(BF)
        return carry

    if inside:
        lax.fori_loop(0, heads // 2, forward, 0, unroll=2)
        pl.semaphore_wait(barrier, 2)
        fetch_cot.start()
        send_cot.start()
        lax.fori_loop(heads // 2, heads, forward, 0, unroll=2)
    else:
        pl.semaphore_wait(barrier, 1)
        send_cot.start()
        send_cot_far.start()
        lax.fori_loop(0, heads, forward, 0, unroll=4)

    loads[5].wait()
    attention = attn_t[...].T
    part_out[0] = dot(attention, w_ref[:, columns(far_peer)]).astype(BF)
    send_part_far.start()
    part_far[...] = dot(attention, w_ref[:, columns(far)])
    part_out[1] = dot(attention, w_ref[:, columns(peer)]).astype(BF)
    send_part_peer.start()
    send_part_far.wait_recv()
    far_out[...] = (part_far[...] + part_in[0].astype(F32)).astype(BF)
    if inside:
        send_far.start()
    part_own[...] = dot(attention, w_ref[:, columns(h)])
    loads[4].wait()
    g_sum[...] = dot_nt(cot_ref[...], w_ref[:, columns(h)])
    send_cot.wait_recv()
    g_sum[...] += dot_nt(cots[0], w_ref[:, columns(peer)])
    send_part_peer.wait_recv()
    part_own[...] += part_in[1].astype(F32)

    if inside:
        fetch_cot.wait_recv()
        send_cot_far.start()
    g_sum[...] += dot_nt(cot_far[...], w_ref[:, columns(far)])
    send_cot_far.wait_recv()
    grad_attention = (g_sum[...] + dot_nt(cots[1], w_ref[:, columns(far_peer)])).astype(BF)
    for head in range(heads):
        mask = jnp.where(lane_head == head, 1.0, 0.0).astype(BF)
        g_stack[head * rows : (head + 1) * rows, :] = grad_attention * mask
    products = grad_attention.T.astype(F32) * attn_t[...].astype(F32)
    delta[...] = jnp.sum(products.reshape(heads, HD, rows), axis=1)

    def backward(head, carry):
        row_delta = delta[pl.ds(head, 1), :]
        for half, values in enumerate((v_ref, mate_v)):
            keys = slice(half * rows, (half + 1) * rows)
            grad_probs = dot_nt(values[...], g_stack[head_rows(head), :])
            grads = probs[head, keys, :] * (grad_probs - row_delta)
            grads_bf[keys, head_rows(head)] = grads.astype(BF)
        lanes = pl.ds(pl.multiple_of(head * HD, HD), HD)
        grads = dot(k_t[lanes, :], grads_bf[:, head_rows(head)])
        dq_t[lanes, :] = (grads * HD**-0.5).astype(BF)
        return carry

    lax.fori_loop(0, heads, backward, 0, unroll=4)
    dq_ref[...] = dq_t[...].T
    dv_cross[...] = dot(probs_bf[rows:, :], g_stack[...]).astype(BF)
    dk_cross[...] = dot(grads_bf[rows:, :], q_stack[...]).astype(BF)
    dv_own[...] = dot(probs_bf[:rows, :], g_stack[...])
    dk_own[...] = dot(grads_bf[:rows, :], q_stack[...])
    if inside:
        send_far.wait_recv()
    for done in sent:
        done.wait_send()


def attend(inside, *operands):
    queries, partner = operands[0], operands[8]
    rows, width = queries.shape
    heads = width // HD
    narrow = jax.ShapeDtypeStruct((rows, width), BF)
    wide = jax.ShapeDtypeStruct((rows, width), F32)
    vmem = pl.BlockSpec(memory_space=pltpu.VMEM)
    anywhere = pl.BlockSpec(memory_space=pl.ANY)
    block = pltpu.VMEM((rows, width), BF)
    scratch = [
        block,
        block,
        block,
        block,
        pltpu.VMEM(operands[7].shape, BF),
        pltpu.SMEM(partner.shape, partner.dtype),
        block,
        pltpu.VMEM((2, rows, width), BF),
        pltpu.VMEM((heads * rows, width), BF),
        pltpu.VMEM((heads * rows, width), BF),
        pltpu.VMEM((width, 2 * rows), BF),
        pltpu.VMEM((width, 2 * rows), BF),
        pltpu.VMEM((heads, 2 * rows, rows), F32),
        pltpu.VMEM((2 * rows, heads * rows), BF),
        pltpu.VMEM((2 * rows, heads * rows), BF),
        pltpu.VMEM((width, rows), BF),
        pltpu.VMEM((width, rows), BF),
        pltpu.VMEM((heads, rows), F32),
        pltpu.VMEM((rows, width), F32),
        pltpu.VMEM((rows, width), F32),
        pltpu.VMEM((2, rows, width), BF),
        pltpu.VMEM((2, rows, width), BF),
        pltpu.SemaphoreType.DMA((6,)),
        pltpu.SemaphoreType.DMA((6,)),
        pltpu.SemaphoreType.DMA((6,)),
    ] + [block] * (2 * inside)
    in_specs = [anywhere] * 3 + [vmem] * 3 + [anywhere] * 3 + [vmem] * (not inside)
    taken, given = len(in_specs), 7

    def body(*refs):
        kernel(inside, refs[:taken], refs[taken : taken + given], refs[taken + given :])

    return pl.pallas_call(
        body,
        out_shape=(wide, narrow, narrow, wide, wide, narrow, narrow),
        in_specs=in_specs,
        out_specs=(vmem,) * given,
        scratch_shapes=scratch,
        compiler_params=pltpu.CompilerParams(
            collective_id=int(inside), has_side_effects=True, vmem_limit_bytes=20 << 20
        ),
        cost_estimate=pl.CostEstimate(
            flops=600_000_000, bytes_accessed=3 << 20, transcendentals=524288
        ),
    )(*operands)


def finish_kernel(
    part_own, far_in, dq, dk_own, dv_own, dk_direct, dk_relayed, dv_in, partner_any,
    lo_out, dq_out, dk_out, dv_out, lo, dk, dv, partner, sems,
):
    load = pltpu.make_async_copy(partner_any, partner, sems.at[0])
    load.start()
    stores = [
        pltpu.make_async_copy(source, target, sems.at[1 + i])
        for i, (source, target) in enumerate(((dq, dq_out), (lo, lo_out), (dv, dv_out), (dk, dk_out)))
    ]
    stores[0].start()
    lo[...] = (part_own[...] + far_in[...].astype(F32)).astype(BF)
    stores[1].start()
    dv[...] = (dv_own[...] + dv_in[...].astype(F32)).astype(BF)
    stores[2].start()
    load.wait()
    dk[...] = (dk_own[...] + choose(partner, dk_direct, dk_relayed).astype(F32)).astype(BF)
    stores[3].start()
    for store in stores:
        store.wait()


def finish(part_own, far_in, dq, dk_own, dv_own, returned, partner):
    vmem = pl.BlockSpec(memory_space=pltpu.VMEM)
    anywhere = pl.BlockSpec(memory_space=pl.ANY)
    return pl.pallas_call(
        finish_kernel,
        out_shape=(jax.ShapeDtypeStruct(dq.shape, BF),) * 4,
        in_specs=[vmem] * 8 + [anywhere],
        out_specs=(anywhere,) * 4,
        scratch_shapes=[pltpu.VMEM(dq.shape, BF)] * 3
        + [pltpu.SMEM(partner.shape, partner.dtype), pltpu.SemaphoreType.DMA((5,))],
        compiler_params=pltpu.CompilerParams(vmem_limit_bytes=4 << 20),
    )(part_own, far_in, dq, dk_own, dv_own, *returned, partner)


PIECES = 2


def near(pair):
    return pair // 2 % 4 == 0


def per_device(queries, key_states, value_states, cotangent, out_weight, partner, counts):
    blocks = partner.shape[0]
    partner = partner + blocks * counts
    pair = partner[0] % blocks // 2
    everything = range(partner.shape[0] // 2)
    near_pairs = [p for p in everything if near(p)]
    long_pairs = [p for p in everything if not near(p)]

    def stay(queries, key_states, value_states, cotangent, out_weight, partner):
        which = pair // 8 * 2 + pair % 2
        *mates, cotangent_far = swap_any(
            near_pairs, which, (key_states, value_states, cotangent), partner
        )
        part_own, far_out, dq, dk_own, dv_own, dk_cross, dv_cross = attend(
            False, queries, key_states, value_states, *mates, cotangent, out_weight, partner,
            cotangent_far,
        )
        *returned, far_in = swap_any(near_pairs, which, (dk_cross, dv_cross, far_out), partner)
        return finish(part_own, far_in, dq, dk_own, dv_own, returned, partner)

    def cross(queries, key_states, value_states, cotangent, out_weight, partner):
        which = (pair // 8 * 3 + pair // 2 % 4 - 1) * 2 + pair % 2
        mates = swap_any(long_pairs, which, (key_states, value_states), partner)
        part_own, far_in, dq, dk_own, dv_own, dk_cross, dv_cross = attend(
            True, queries, key_states, value_states, *mates, cotangent, out_weight, partner
        )
        returned = swap_any(long_pairs, which, (dk_cross, dv_cross), partner)
        return finish(part_own, far_in, dq, dk_own, dv_own, returned, partner)

    operands = queries, key_states, value_states, cotangent, out_weight, partner
    if not long_pairs:
        return stay(*operands)
    return lax.cond(near(pair), stay, cross, *operands)


def solution(mesh):
    return jax.shard_map(
        per_device,
        mesh=mesh,
        in_specs=(
            P("seq", "head"), P("seq", "head"), P("seq", "head"), P("seq", "head"),
            P("head", None), P(), P(),
        ),
        out_specs=(P("seq", "head"),) * 4,
        check_vma=False,
    )
```
